128 devices in a mesh: tok: 16 (over y, x_hi, core), src: 8 (over x_lo, z).
Axes of the slice: x: 4 (x_hi: 2, x_lo: 2; x = x_hi * 2 + x_lo), y: 4, z: 4, core: 2. Of those that a mesh axis runs over, the one named last changes fastest.
Arguments:
- hidden_in: bfloat16 [32768, 1024], P(('tok', 'src')), may hold values from -24 to 24
- d_out: bfloat16 [32768, 1024], P(('tok', 'src')), may hold values from -6 to 6
- queries: bfloat16 [32768, 1024], P(('tok', 'src')), may hold values from -160 to 160
- keys: bfloat16 [16, 1024, 1024], P('tok', 'src'), may hold values from -6 to 6
- values: bfloat16 [16, 1024, 1024], P('tok', 'src'), may hold values from -6 to 6
- source_len: int32 [16], replicated, may hold values from 256 to 1024, as said below
- out_weight: bfloat16 [1024, 1024], replicated, may hold values from -0.1875 to 0.1875
- norm_gain: float32 [1024], replicated, may hold values from 0.25 to 1.75
- router: bfloat16 [1024, 128], replicated, may hold values from -0.1875 to 0.1875
- expert_ids: int32 [32768, 2], P(('tok', 'src')), may hold values from 0 to 127, as said below
- expert_slots: int32 [32768, 2], P(('tok', 'src')), may hold values from -1 to 3, as said below
- fc_in: bfloat16 [16, 4096, 1024], P('tok', 'src'), may hold values from -0.1875 to 0.1875
- fc_out: bfloat16 [16, 4096, 1024], P('tok', 'src'), may hold values from -0.09375 to 0.09375
Outputs:
- d_hidden: bfloat16 [32768, 1024], P(('tok', 'src'))
- d_queries: bfloat16 [32768, 1024], P(('tok', 'src'))
- d_keys: bfloat16 [16, 1024, 1024], P('tok', 'src')
- d_values: bfloat16 [16, 1024, 1024], P('tok', 'src')
- d_out_weight: float32 [1024, 1024], P(('tok', 'src'))
- d_router: float32 [1024, 128], replicated
- d_gain: float32 [1024], replicated
- d_fc_in: bfloat16 [16, 4096, 1024], P('tok', 'src')
- d_fc_out: bfloat16 [16, 4096, 1024], P('tok', 'src')
The draws below stay inside these ranges and needn't reach their ends.
Inputs may be any that keep to these rules, and one draw needn't show every extreme that they name: `source_len`: each document has at least one live source position; the longest document is full and the shortest has 256 positions. `expert_ids`: the two numbers of a token differ; numbers below 16 are the window's experts. `expert_slots`: for a choice of an expert e below 16: its rank among the choices of e made by the 256 tokens of the same device (tokens in order, a token's first choice before its second), or -1 when that rank is 4 or more; -1 for experts outside the window.
All inputs are finite; a program needn't handle non-finite values.
Results may differ from the reference program's by a relative error of at most 0.019.
Values may be sent and summed in bfloat16 or wider, within the bound.
A program may use at most 128 MiB of HBM per device.

```python
import math
import jax
import jax.numpy as jnp
from jax import lax

D = 1024
FF = 4096
HEAD_DIM = 128
EXPERTS_ALL = 128
HEADS = 8
CAP = 4
TOK_DEV = 256
WIN = 16
DOCS = 16
SRC_LEN = 1024
TOKENS = 32768
N_TOK = 16


def key_field(key):
    field = jax.random.normal(jax.random.fold_in(key, 101), (DOCS, SRC_LEN, HEADS * HEAD_DIM), jnp.float32)
    return jnp.clip(field, -6.0, 6.0)


def draw_keys(key, part):
    field = key_field(key)
    return field.astype(jnp.bfloat16)


def draw_queries(key, part):
    key = jax.random.fold_in(key, 2)
    drawn_rows = jnp.clip(jax.random.normal(key, (TOKENS, HEADS * HEAD_DIM), jnp.float32), -6.0, 6.0)
    return drawn_rows.astype(jnp.bfloat16)


def draw_source_len(key, part):
    key = jax.random.fold_in(key, 4)
    key_lens, key_long, key_short = jax.random.split(key, 3)
    lengths = jax.random.randint(key_lens, (DOCS,), SRC_LEN // 4, SRC_LEN + 1)
    longest = jax.random.randint(key_long, (), 0, DOCS)
    shortest = (longest + jax.random.randint(key_short, (), 1, DOCS)) % DOCS
    doc_ids = jnp.arange(DOCS)
    lengths = jnp.where(doc_ids == longest, SRC_LEN, lengths)
    lengths = jnp.where(doc_ids == shortest, SRC_LEN // 4, lengths)
    return lengths.astype(jnp.int32)


def route_draw(key):
    key = jax.random.fold_in(key, 200)
    key_first, key_hot, key_shuffle, key_offset = jax.random.split(key, 4)
    blocks = TOKENS // TOK_DEV
    first_ids = jax.random.randint(key_first, (TOKENS,), 0, EXPERTS_ALL)
    hot_expert = jax.random.randint(key_hot, (), 0, WIN)
    shuffled = jax.vmap(lambda one_key: jax.random.permutation(one_key, TOK_DEV))(jax.random.split(key_shuffle, blocks))
    forced = (shuffled < CAP).reshape(TOKENS)
    first_ids = jnp.where(forced, hot_expert, first_ids)
    second = (first_ids + jax.random.randint(key_offset, (TOKENS,), 1, EXPERTS_ALL)) % EXPERTS_ALL
    id_pairs = jnp.stack([first_ids, second], axis=1).astype(jnp.int32)
    flat_ids = id_pairs.reshape(blocks, TOK_DEV * 2)
    onehot = (flat_ids[:, :, None] == jnp.arange(WIN)[None, None, :]).astype(jnp.int32)
    rank_all = jnp.cumsum(onehot, axis=1) - onehot
    own_rank = jnp.sum(rank_all * onehot, axis=2)
    in_window = flat_ids < WIN
    slot_ids = jnp.where(in_window & (own_rank < CAP), own_rank, -1)
    return (id_pairs, slot_ids.reshape(TOKENS, 2).astype(jnp.int32))


def draw_expert_ids(key, part):
    id_pairs, slot_ids = route_draw(key)
    return id_pairs


def draw_expert_slots(key, part):
    id_pairs, slot_ids = route_draw(key)
    return slot_ids


def spiked(drawn, stream_key, source, target, parts, factor):
    def block_of(position):
        return (jnp.arange(drawn.shape[position]) // (drawn.shape[position] // parts)).reshape((-1,) + (1,) * (drawn.ndim - 1 - position))

    near = jax.random.permutation(stream_key, parts)[block_of(target)]
    other_side = (block_of(target) + parts // 2) % parts
    return jnp.where((block_of(source) == near) | (block_of(source) == other_side), factor * drawn, drawn)


def block_scale(own_key, dims, shards, low, largest):
    factor_of = 1.0
    for axis_at, parts in shards:
        steps = jax.random.uniform(jax.random.fold_in(jax.random.fold_in(own_key, 6), axis_at), (parts,), jnp.float32, low / len(shards), largest / len(shards))
        factor_of = factor_of * jnp.repeat(jnp.exp(steps), dims[axis_at] // parts).reshape((-1,) + (1,) * (len(dims) - 1 - axis_at))
    return factor_of


def normal_values(own_key, extent, deviation, bound, cuts=(), held_as=jnp.bfloat16):
    array = deviation * jax.random.normal(own_key, extent, jnp.float32)
    if cuts:
        array = array * block_scale(own_key, extent, cuts, -0.22, 0.18)
    return jnp.clip(array, -bound, bound).astype(held_as)


def noise_with(stream_key, dims, deviation, reach, shards, heavy, kind=jnp.bfloat16):
    values = deviation * jax.random.normal(stream_key, dims, jnp.float32)
    if shards:
        values = values * block_scale(stream_key, dims, shards, -0.22, 0.18)
    return jnp.clip(spiked(values, jax.random.fold_in(stream_key, 3), *heavy), -reach, reach).astype(kind)


def setup_inputs(seed: int = 0) -> dict:
    splits = jax.random.split(jax.random.key(seed), 14)
    return {
        "hidden_in": noise_with(splits[0], (TOKENS, D), 1.0, 24.0, ((0, 128),), (0, 1, 128, 5.5)),
        "d_out": normal_values(splits[1], (TOKENS, D), 1.0, 6.0, ((0, 128),)),
        "queries": draw_queries(jax.random.fold_in(splits[13], 71), 0),
        "keys": draw_keys(jax.random.fold_in(splits[13], 71), 0),
        "values": normal_values(splits[4], (DOCS, SRC_LEN, HEADS * HEAD_DIM), 1.0, 6.0, ((0, 16), (1, 8))),
        "source_len": draw_source_len(jax.random.fold_in(splits[13], 71), 0),
        "out_weight": normal_values(splits[6], (HEADS * HEAD_DIM, D), (HEADS * HEAD_DIM) ** -0.5, 0.1875),
        "norm_gain": jnp.clip(1.0 + 0.15 * jax.random.normal(splits[7], (D,), jnp.float32), 0.25, 1.75),
        "router": normal_values(splits[8], (D, EXPERTS_ALL), D ** -0.5, 0.1875),
        "expert_ids": draw_expert_ids(jax.random.fold_in(splits[13], 71), 0),
        "expert_slots": draw_expert_slots(jax.random.fold_in(splits[13], 71), 0),
        "fc_in": normal_values(splits[11], (WIN, FF, D), D ** -0.5, 0.1875, ((0, 16), (1, 8))),
        "fc_out": normal_values(splits[12], (WIN, FF, D), FF ** -0.5, 0.09375, ((0, 16), (1, 8))),
    }


MASKED = -1e+30
NORM_EPS = 1e-05
GELU_SCALE = 0.7978845608028654
CUBIC_TERM = 0.044715

def gelu_pair(pre_act):
    tangent = jnp.tanh(GELU_SCALE * (pre_act + CUBIC_TERM * pre_act * pre_act * pre_act))
    gelu_value = 0.5 * pre_act * (1.0 + tangent)
    gelu_slope = 0.5 * (1.0 + tangent) + 0.5 * pre_act * (1.0 - tangent * tangent) * GELU_SCALE * (1.0 + 3.0 * CUBIC_TERM * pre_act * pre_act)
    return (gelu_value, gelu_slope)

def soft_weights(query_doc, key_doc, length):
    query_heads = query_doc.astype(jnp.float32).reshape(-1, HEADS, HEAD_DIM)
    key_heads = key_doc.astype(jnp.float32).reshape(-1, HEADS, HEAD_DIM)
    visible = (jnp.arange(key_heads.shape[0]) < length)[None, None, :]
    scores = jnp.einsum('thd,shd->hts', query_heads, key_heads) * (1.0 / math.sqrt(HEAD_DIM))
    scores = jnp.where(visible, scores, MASKED)
    row_top = lax.optimization_barrier(jnp.max(scores, axis=2, keepdims=True))
    raised = jnp.where(visible, jnp.exp(scores - row_top), 0.0)
    return raised / lax.optimization_barrier(jnp.sum(raised, axis=2, keepdims=True))

def attend_doc(inputs):
    query_doc, key_doc, value_doc, length = inputs
    probs_low = lax.optimization_barrier(soft_weights(query_doc, key_doc, length).astype(jnp.bfloat16))
    value_heads = value_doc.astype(jnp.float32).reshape(-1, HEADS, HEAD_DIM)
    mixed_heads = jnp.einsum('hts,shd->thd', probs_low.astype(jnp.float32), value_heads)
    return mixed_heads.astype(jnp.bfloat16).reshape(query_doc.shape[0], -1)

def attend_back(inputs):
    query_doc, key_doc, value_doc, length, grad_doc, mixed_doc = inputs
    factor = 1.0 / math.sqrt(HEAD_DIM)
    probs_full = soft_weights(query_doc, key_doc, length)
    probs_low = lax.optimization_barrier(probs_full.astype(jnp.bfloat16)).astype(jnp.float32)
    query_heads = query_doc.astype(jnp.float32).reshape(-1, HEADS, HEAD_DIM)
    key_heads = key_doc.astype(jnp.float32).reshape(-1, HEADS, HEAD_DIM)
    value_heads = value_doc.astype(jnp.float32).reshape(-1, HEADS, HEAD_DIM)
    grad_heads = grad_doc.astype(jnp.float32).reshape(-1, HEADS, HEAD_DIM)
    mixed_heads = mixed_doc.astype(jnp.float32).reshape(-1, HEADS, HEAD_DIM)
    row_term = jnp.einsum('thd,thd->ht', grad_heads, mixed_heads)
    prob_grad = jnp.einsum('thd,shd->hts', grad_heads, value_heads)
    score_grad = (probs_full * (prob_grad - row_term[:, :, None]) * factor).astype(jnp.bfloat16)
    score_wide = lax.optimization_barrier(score_grad).astype(jnp.float32)
    d_query = jnp.einsum('hts,shd->thd', score_wide, key_heads).astype(jnp.bfloat16)
    d_key = jnp.einsum('hts,thd->shd', score_wide, query_heads).astype(jnp.bfloat16)
    d_value = jnp.einsum('hts,thd->shd', probs_low, grad_heads).astype(jnp.bfloat16)
    return (d_query.reshape(query_doc.shape[0], -1), d_key.reshape(key_doc.shape[0], -1), d_value.reshape(key_doc.shape[0], -1))

def reference(hidden_in, d_out, queries, keys, values, source_len, out_weight, norm_gain, router, expert_ids, expert_slots, fc_in, fc_out):
    tok_total = hidden_in.shape[0]
    query_docs = queries.reshape(N_TOK, -1, queries.shape[1])
    attended = lax.map(attend_doc, (query_docs, keys, values, source_len)).reshape(tok_total, -1)
    mixed = hidden_in.astype(jnp.float32) + jnp.dot(attended, out_weight, preferred_element_type=jnp.float32)
    row_mean = lax.optimization_barrier(jnp.mean(mixed, axis=1, keepdims=True))
    centred = mixed - row_mean
    inv_std = lax.rsqrt(lax.optimization_barrier(jnp.mean(centred * centred, axis=1, keepdims=True)) + NORM_EPS)
    normed = centred * inv_std
    expert_in = (normed * norm_gain).astype(jnp.bfloat16)
    logits = jnp.dot(expert_in, router, preferred_element_type=jnp.float32)
    first_logit = jnp.take_along_axis(logits, expert_ids[:, 0:1], axis=1)[:, 0]
    second_logit = jnp.take_along_axis(logits, expert_ids[:, 1:2], axis=1)[:, 0]
    first_gate = jax.nn.sigmoid(first_logit - second_logit)
    second_gate = jax.nn.sigmoid(second_logit - first_logit)
    gates_low = lax.optimization_barrier(jnp.stack([first_gate, second_gate], axis=1).astype(jnp.bfloat16))
    gates_low = gates_low.astype(jnp.float32)
    owner_dev = (jnp.arange(tok_total) // TOK_DEV).astype(jnp.int32)
    token_numbers = jnp.arange(tok_total).astype(jnp.int32)
    width_slots = tok_total // TOK_DEV * CAP

    def window_place(id_col, slot_col):
        is_live = (id_col < WIN) & (slot_col >= 0)
        expert_row = jnp.where(is_live, id_col, WIN).astype(jnp.int32)
        slot_place = (owner_dev * CAP + jnp.maximum(slot_col, 0)).astype(jnp.int32)
        return (is_live, expert_row, slot_place)
    live_first, row_first, place_first = window_place(expert_ids[:, 0], expert_slots[:, 0])
    live_second, row_second, place_second = window_place(expert_ids[:, 1], expert_slots[:, 1])
    slot_table = jnp.full((WIN, width_slots), tok_total, jnp.int32)
    slot_table = slot_table.at[row_first, place_first].set(token_numbers, mode='drop')
    slot_table = slot_table.at[row_second, place_second].set(token_numbers, mode='drop')
    gate_table = jnp.zeros((WIN, width_slots), jnp.float32)
    gate_table = gate_table.at[row_first, place_first].set(gates_low[:, 0], mode='drop')
    gate_table = gate_table.at[row_second, place_second].set(gates_low[:, 1], mode='drop')
    padded_in = jnp.concatenate([expert_in, jnp.zeros((1, D), jnp.bfloat16)], axis=0)
    padded_grad = jnp.concatenate([d_out, jnp.zeros((1, D), jnp.bfloat16)], axis=0)

    def one_expert(inputs):
        token_rows, gate_col, weight_in, weight_out = inputs
        rows_in = padded_in[token_rows]
        rows_grad = padded_grad[token_rows]
        gate_rows = gate_col[:, None]
        pre_act = jnp.dot(rows_in, weight_in.T, preferred_element_type=jnp.float32)
        gelu_value, gelu_slope = gelu_pair(pre_act)
        activated = lax.optimization_barrier(gelu_value.astype(jnp.bfloat16))
        back_proj = jnp.dot(rows_grad, weight_out.T, preferred_element_type=jnp.float32)
        gate_part = lax.optimization_barrier(jnp.sum(back_proj * activated.astype(jnp.float32), axis=1))
        d_pre = (gate_rows * back_proj * gelu_slope).astype(jnp.bfloat16)
        scaled_grad = (gate_rows * rows_grad.astype(jnp.float32)).astype(jnp.bfloat16)
        d_weight_out = jnp.dot(activated.T, scaled_grad, preferred_element_type=jnp.float32).astype(jnp.bfloat16)
        d_weight_in = jnp.dot(d_pre.T, rows_in, preferred_element_type=jnp.float32).astype(jnp.bfloat16)
        input_part = jnp.dot(d_pre, weight_in, preferred_element_type=jnp.float32)
        return (d_weight_in, d_weight_out, input_part, gate_part)
    d_fc_in, d_fc_out, input_rows, gate_rows_all = lax.map(one_expert, (slot_table, gate_table, fc_in, fc_out))
    moe_grad = jnp.zeros((tok_total + 1, D), jnp.float32).at[slot_table.reshape(-1)].add(input_rows.reshape(-1, D))[:tok_total]
    grad_first = jnp.where(live_first, gate_rows_all[jnp.minimum(row_first, WIN - 1), place_first], 0.0)
    grad_second = jnp.where(live_second, gate_rows_all[jnp.minimum(row_second, WIN - 1), place_second], 0.0)
    logit_grad = first_gate * second_gate * (grad_first - grad_second)
    columns = jnp.arange(EXPERTS_ALL)
    pick_first = (expert_ids[:, 0:1] == columns).astype(jnp.float32)
    pick_second = (expert_ids[:, 1:2] == columns).astype(jnp.float32)
    column_grad = (pick_first - pick_second) * logit_grad[:, None]
    total_grad = moe_grad + jnp.dot(column_grad, router.astype(jnp.float32).T, precision=lax.Precision.HIGHEST)
    d_router = jnp.dot(expert_in.astype(jnp.float32).T, column_grad, precision=lax.Precision.HIGHEST)
    d_gain = lax.optimization_barrier(jnp.sum(total_grad * normed, axis=0))
    scaled = total_grad * norm_gain
    mixed_grad = d_out.astype(jnp.float32) + inv_std * (scaled - lax.optimization_barrier(jnp.mean(scaled, axis=1, keepdims=True)) - normed * lax.optimization_barrier(jnp.mean(scaled * normed, axis=1, keepdims=True)))
    d_hidden = mixed_grad.astype(jnp.bfloat16)
    out_grad = jnp.dot(d_hidden, out_weight.T, preferred_element_type=jnp.float32).astype(jnp.bfloat16)
    d_out_weight = jnp.dot(attended.T, d_hidden, preferred_element_type=jnp.float32)
    grad_docs = out_grad.reshape(N_TOK, -1, out_grad.shape[1])
    attended_docs = attended.reshape(N_TOK, -1, attended.shape[1])
    d_query_docs, d_keys, d_values = lax.map(attend_back, (query_docs, keys, values, source_len, grad_docs, attended_docs))
    d_queries = d_query_docs.reshape(tok_total, -1)
    return (d_hidden, d_queries, d_keys, d_values, d_out_weight, d_router, d_gain, d_fc_in, d_fc_out)
```

```python
import math

import jax
import jax.numpy as jnp
from jax import lax
from jax.experimental import pallas as pl
from jax.experimental.pallas import tpu as pltpu
from jax.sharding import PartitionSpec as P

MESH = pl.DeviceIdType.MESH
BF, F32 = jnp.bfloat16, jnp.float32
HEAD = 128
CAP = 4
NORM_EPS = 1e-05
GELU_SCALE = 0.7978845608028654
CUBIC_TERM = 0.044715
FACTOR = 1.0 / math.sqrt(HEAD)
EXP2_SCALE = FACTOR / math.log(2.0)
MASKED = -1e30
N_SRC, N_TOK = 8, 16
ROWS, WIDTH, SRC_ALL = 256, 1024, 1024


def nn(a, b, **kw):
    return lax.dot_general(a, b, (((1,), (0,)), ((), ())), preferred_element_type=F32, **kw)


def nt(a, b, **kw):
    return lax.dot_general(a, b, (((1,), (1,)), ((), ())), preferred_element_type=F32, **kw)


def src_step(src, k, back=False):
    x, z = src // 4, src % 4
    z = (z + 4 - k % 4) % 4 if back else (z + k % 4) % 4
    return ((x + k // 4) % 2) * 4 + z


def tok_step(tok, k, back=False):
    y, x, c = tok // 4, (tok // 2) % 2, tok % 2
    y = (y + 4 - k // 4) % 4 if back else (y + k // 4) % 4
    return y * 4 + ((x + (k // 2) % 2) % 2) * 2 + (c + k % 2) % 2


def remote(src_ref, dst_ref, send_sem, recv_sem, axis, peer):
    return pltpu.make_async_remote_copy(
        src_ref=src_ref,
        dst_ref=dst_ref,
        send_sem=send_sem,
        recv_sem=recv_sem,
        device_id={axis: peer},
        device_id_type=MESH,
    )


def each(count, body):
    def step(k, carry):
        body(k)
        return carry

    lax.fori_loop(1, count, step, 0)


def greet(src, tok):
    bar = pltpu.get_barrier_semaphore()
    waits = 0
    if src is not None:
        waits += N_SRC - 1
        each(N_SRC, lambda k: pl.semaphore_signal(bar, inc=1, device_id={"src": src_step(src, k)}, device_id_type=MESH))
    if tok is not None:
        waits += N_TOK - 1
        each(N_TOK, lambda k: pl.semaphore_signal(bar, inc=1, device_id={"tok": tok_step(tok, k)}, device_id_type=MESH))
    pl.semaphore_wait(bar, waits)


class Swap:
    def __init__(self, axis, me, sems, source, target):
        self.axis, self.me, self.sems = axis, me, sems
        self.source, self.target = source, target
        self.count = N_SRC if axis == "src" else N_TOK
        self.step = src_step if axis == "src" else tok_step

    def copy(self, k, to, slot):
        return remote(self.source(to), self.target(slot), self.sems.at[0, k], self.sems.at[1, k], self.axis, to)

    def send(self, k):
        self.copy(k, self.step(self.me, k), self.me).start()

    def arrive(self, k):
        sender = self.step(self.me, k, True)
        self.copy(k, sender, sender).wait_recv()

    def sent(self, k):
        self.copy(k, self.step(self.me, k), self.me).wait_send()

    def send_all(self):
        each(self.count, self.send)

    def arrive_all(self):
        each(self.count, self.arrive)

    def sent_all(self):
        each(self.count, self.sent)


def lanes(index):
    return pl.ds(pl.multiple_of(index * HEAD, HEAD), HEAD)


def rows(index, size):
    return pl.ds(pl.multiple_of(index * size, size), size)


def fill_bias(length, bias):
    place = lax.broadcasted_iota(jnp.int32, bias.shape, 0)
    bias[...] = jnp.where(place < length, 0.0, MASKED)


def fold8(value, op):
    return op(value.reshape(value.shape[0] // 8, 8, value.shape[1]), axis=0)


def attend_kernel(
    q_ref, k_ref, v_ref, len_ref,
    att_out, qh_out, kh_out, vh_out, oT_out, stat_out,
    qh, kh, vh, att_in, att_send, vT, sbuf, pbuf, bias,
    k_sem, v_sem, q_sem, a_sem,
):
    src, tok = lax.axis_index("src"), lax.axis_index("tok")
    greet(src, None)
    k_swap = Swap("src", src, k_sem, lambda p: k_ref.at[:, lanes(p)], lambda i: kh.at[rows(i, 128)])
    v_swap = Swap("src", src, v_sem, lambda p: v_ref.at[:, lanes(p)], lambda i: vh.at[rows(i, 128)])
    q_swap = Swap("src", src, q_sem, lambda p: q_ref.at[:, lanes(p)], lambda i: qh.at[i])
    a_swap = Swap("src", src, a_sem, lambda p: att_send.at[p], lambda i: att_in.at[i])
    k_swap.send_all()
    v_swap.send_all()
    q_swap.send_all()
    kh[rows(src, 128), :] = k_ref[:, lanes(src)]
    vh[rows(src, 128), :] = v_ref[:, lanes(src)]
    qh[src] = q_ref[:, lanes(src)]
    fill_bias(len_ref[tok], bias)
    k_swap.arrive_all()
    v_swap.arrive_all()
    vT[...] = vh[...].astype(F32).T.astype(BF)

    def block(b):
        q = qh[b]
        top = jnp.full((8, ROWS), -3e38, F32)
        for c in range(0, SRC_ALL, 128):
            s = nt(kh[c : c + 128, :], q) + bias[c : c + 128, :]
            sbuf[c : c + 128, :] = s
            top = jnp.maximum(top, fold8(s, jnp.max))
        top = jnp.max(top, axis=0, keepdims=True)
        total = jnp.zeros((8, ROWS), F32)
        for c in range(0, SRC_ALL, 128):
            p = jnp.exp2((sbuf[c : c + 128, :] - top) * EXP2_SCALE)
            total = total + fold8(p, jnp.sum)
            pbuf[c : c + 128, :] = p.astype(BF)
        inv = 1.0 / jnp.sum(total, axis=0, keepdims=True)
        oT = nn(vT[...], pbuf[...]) * inv
        oT_out[b] = oT.astype(BF)
        stat_out[b] = jnp.concatenate([jnp.broadcast_to(top, (8, ROWS)), jnp.broadcast_to(inv, (8, ROWS))], axis=0)
        att_send[b] = oT.T.astype(BF)

    block(src)
    att_in[src] = att_send[src]

    def later(k):
        q_swap.arrive(k)
        b = src_step(src, k, True)
        block(b)
        back = src_step(0, k, True)
        a_swap.send(back)

    each(N_SRC, later)
    qh_out[...] = qh[...]
    kh_out[...] = kh[...]
    vh_out[...] = vh[...]
    a_swap.arrive_all()
    for h in range(N_SRC):
        att_out[:, h * HEAD : (h + 1) * HEAD] = att_in[h]
    k_swap.sent_all()
    v_swap.sent_all()
    q_swap.sent_all()
    a_swap.sent_all()


def gelu_pair(x):
    k = jnp.tanh(GELU_SCALE * (x + CUBIC_TERM * x * x * x))
    value = 0.5 * x * (1.0 + k)
    slope = 0.5 * (1.0 + k) + 0.5 * x * (1.0 - k * k) * GELU_SCALE * (1.0 + 3.0 * CUBIC_TERM * x * x)
    return value, slope


def iota(shape, dim):
    return lax.broadcasted_iota(jnp.int32, shape, dim)


def expert_kernel(
    att, hid, dout, w_out, gain, router, ids, slots, f_in, f_out,
    dhid, og, d_fin, d_fout, r_part, g_part,
    mixed, xin, hit_f, hitT, xs, gs, ms, xr, gr, mr, xall, gall, mall,
    actg, dpT, dpr, part, pr, gps, gpr, ps, br, gsum, gb,
    x_sem, g_sem, m_sem, xa_sem, ga_sem, ma_sem, p_sem, gp_sem, b_sem, gb_sem,
):
    src, tok = lax.axis_index("src"), lax.axis_index("tok")
    greet(src, tok)
    x_swap = Swap("tok", tok, x_sem, lambda p: xs.at[rows(p, 16)], lambda i: xr.at[rows(i, 16)])
    g_swap = Swap("tok", tok, g_sem, lambda p: gs.at[rows(p, 16)], lambda i: gr.at[rows(i, 16)])
    m_swap = Swap("tok", tok, m_sem, lambda p: ms.at[rows(p, 8)], lambda i: mr.at[rows(i, 8)])
    xa_swap = Swap("src", src, xa_sem, lambda p: xall.at[rows(src, 64)], lambda i: xall.at[rows(i, 64)])
    ga_swap = Swap("src", src, ga_sem, lambda p: gall.at[rows(src, 64)], lambda i: gall.at[rows(i, 64)])
    ma_swap = Swap("src", src, ma_sem, lambda p: mall.at[src], lambda i: mall.at[i])
    p_swap = Swap("src", src, p_sem, lambda p: part.at[rows(p, 64)], lambda i: pr.at[i])
    gp_swap = Swap("src", src, gp_sem, lambda p: gps.at[p // 2], lambda i: gpr.at[i])
    b_swap = Swap("tok", tok, b_sem, lambda p: ps.at[rows(p, 16)], lambda i: br.at[rows(i, 16)])
    gb_swap = Swap("tok", tok, gb_sem, lambda p: gsum, lambda i: gb.at[rows(i, 8)])

    id1, id2 = ids[:, 0:1], ids[:, 1:2]
    slot1, slot2 = slots[:, 0:1], slots[:, 1:2]
    live1 = (id1 < N_TOK) & (slot1 >= 0)
    live2 = (id2 < N_TOK) & (slot2 >= 0)
    aim1 = jnp.where(live1, id1 * CAP + slot1, -1)
    aim2 = jnp.where(live2, id2 * CAP + slot2, -1)
    j = iota((ROWS, ROWS), 1)
    key = (j // 16) * CAP + j % CAP
    hit = jnp.where((aim1 == key) | (aim2 == key), 1.0, 0.0)
    hit_f[...] = hit.astype(BF)
    hitT[...] = hit.T.astype(BF)
    row_blk = (iota((ROWS, ROWS), 0) // CAP) % 4
    col_blk = (j // CAP) % 4
    zero = jnp.zeros((ROWS, ROWS), BF)

    def to_experts(ref, out):
        acc = None
        for b in range(4):
            term = nn(jnp.where(row_blk == b, hitT[...], zero), ref[:, b * 256 : (b + 1) * 256])
            acc = term if acc is None else acc + term
        out[...] = acc.astype(BF)

    to_experts(dout, gs)
    g_swap.send_all()
    gr[rows(tok, 16), :] = gs[rows(tok, 16), :]

    mixed[...] = hid[...].astype(F32) + nn(att[...], w_out[...])
    inv_parts = []
    for r in range(0, ROWS, 64):
        m = mixed[r : r + 64, :]
        centred = m - jnp.mean(m, axis=1, keepdims=True)
        inv = lax.rsqrt(jnp.mean(centred * centred, axis=1, keepdims=True) + NORM_EPS)
        inv_parts.append(inv)
        normed = centred * inv
        mixed[r : r + 64, :] = normed
        xin[r : r + 64, :] = (normed * gain[...]).astype(BF)
    inv_std = jnp.concatenate(inv_parts, axis=0)
    logits = nn(xin[...], router[...])
    lane = iota((ROWS, HEAD), 1)
    pick1 = jnp.where(id1 == lane, 1.0, 0.0)
    pick2 = jnp.where(id2 == lane, 1.0, 0.0)
    gap = jnp.sum(logits * (pick1 - pick2), axis=1, keepdims=True)
    gate1 = 1.0 / (1.0 + jnp.exp(-gap))
    gate2 = 1.0 / (1.0 + jnp.exp(gap))
    low1 = gate1.astype(BF).astype(F32)
    low2 = gate2.astype(BF).astype(F32)

    to_experts(xin, xs)
    x_swap.send_all()
    xr[rows(tok, 16), :] = xs[rows(tok, 16), :]
    base = (src % 2) * 64 + tok * CAP
    own1 = jnp.where(live1 & (id1 == lane // 8), 1.0, 0.0)
    own2 = jnp.where(live2 & (id2 == lane // 8), 1.0, 0.0)
    at1 = jnp.where(lane == base + slot1, 1.0, 0.0)
    at2 = jnp.where(lane == base + slot2, 1.0, 0.0)
    ms[...] = nn((own1 * low1).T.astype(BF), at1.astype(BF)) + nn((own2 * low2).T.astype(BF), at2.astype(BF))
    m_swap.send_all()
    mr[rows(tok, 8), :] = ms[rows(tok, 8), :]

    i64, j256 = iota((64, ROWS), 0), iota((64, ROWS), 1)
    take = [jnp.where(j256 == (i64 // CAP) * 16 + b * CAP + i64 % CAP, 1.0, 0.0).astype(BF) for b in range(4)]

    def unpack(got, out):
        for b in range(4):
            out[rows(src, 64), b * 256 : (b + 1) * 256] = nn(take[b], got[...]).astype(BF)

    g_swap.arrive_all()
    unpack(gr, gall)
    ga_swap.send_all()
    x_swap.arrive_all()
    unpack(xr, xall)
    xa_swap.send_all()
    m_swap.arrive_all()
    mall[src] = fold8(mr[...], jnp.sum)
    ma_swap.send_all()
    ga_swap.arrive_all()
    xa_swap.arrive_all()
    ma_swap.arrive_all()
    gate_row = jnp.concatenate([mall[2 * i][0:1, :] + mall[2 * i + 1][0:1, :] for i in range(4)], axis=1)

    gate_acc = jnp.zeros((8, 512), F32)
    for c in range(0, 512, 128):
        pre = nt(f_in[c : c + 128, :], xall[...])
        value, slope = gelu_pair(pre)
        act = value.astype(BF).astype(F32)
        back = nt(f_out[c : c + 128, :], gall[...])
        gate_acc = gate_acc + fold8(back * act, jnp.sum)
        actg[c : c + 128, :] = (act * gate_row).astype(BF)
        dp = gate_row * back * slope
        dpT[c : c + 128, :] = dp.astype(BF)
        dpr[:, c : c + 128] = dp.T.astype(BF)
    gate_tot = jnp.sum(gate_acc, axis=0, keepdims=True)
    for i in range(4):
        gps[i] = jnp.broadcast_to(gate_tot[:, i * HEAD : (i + 1) * HEAD], (8, HEAD))
    gp_swap.send_all()
    for r in range(0, 512, 256):
        part[r : r + 256, :] = nn(dpr[r : r + 256, :], f_in[...]).astype(BF)
    p_swap.send_all()
    pr[src] = part[rows(src, 64), :]
    gpr[src] = gps[src // 2]
    for c in range(0, 512, 128):
        d_fin[c : c + 128, :] = nn(dpT[c : c + 128, :], xall[...]).astype(BF)
        d_fout[c : c + 128, :] = nn(actg[c : c + 128, :], gall[...]).astype(BF)
    p_swap.arrive_all()
    gp_swap.arrive_all()
    gsum[...] = jnp.sum(gpr[...], axis=0)
    gb_swap.send_all()
    gb[rows(tok, 8), :] = gsum[...]
    acc = None
    for b in range(4):
        blk = jnp.sum(pr[:, :, b * 256 : (b + 1) * 256].astype(F32), axis=0).astype(BF)
        term = nn(take[b].astype(F32).T.astype(BF), blk)
        acc = term if acc is None else acc + term
    ps[...] = acc.astype(BF)
    b_swap.send_all()
    br[rows(tok, 16), :] = ps[rows(tok, 16), :]

    gb_swap.arrive_all()
    first = jnp.where(lane % 8 == 0, 1.0, 0.0)
    got1 = nn(own1 * first, gb[...], precision=lax.Precision.HIGHEST)
    got2 = nn(own2 * first, gb[...], precision=lax.Precision.HIGHEST)
    grad1 = jnp.sum(got1 * at1, axis=1, keepdims=True)
    grad2 = jnp.sum(got2 * at2, axis=1, keepdims=True)
    logit_grad = gate1 * gate2 * (grad1 - grad2)
    column = (pick1 - pick2) * logit_grad
    col_hi = column.astype(BF)
    col_lo = (column - col_hi.astype(F32)).astype(BF)
    colT = column.T
    colT_hi = colT.astype(BF)
    colT_lo = (colT - colT_hi.astype(F32)).astype(BF)
    r_part[...] = (nn(colT_hi, xin[...]) + nn(colT_lo, xin[...])).T
    b_swap.arrive_all()
    gain_rows = []
    scaled_sum = jnp.zeros((ROWS, 1), F32)
    cross_sum = jnp.zeros((ROWS, 1), F32)
    scaled_all = []
    for b in range(4):
        cut = slice(b * 256, (b + 1) * 256)
        total = nn(jnp.where(col_blk == b, hit_f[...], zero), br[...])
        total = total + nt(col_hi, router[cut, :]) + nt(col_lo, router[cut, :])
        normed = mixed[:, cut]
        row = jnp.sum(total * normed, axis=0, keepdims=True)
        gain_rows += [row[:, :HEAD], row[:, HEAD:]]
        scaled = total * gain[:, cut]
        scaled_all.append(scaled)
        scaled_sum = scaled_sum + jnp.sum(scaled, axis=1, keepdims=True)
        cross_sum = cross_sum + jnp.sum(scaled * normed, axis=1, keepdims=True)
    g_part[...] = jnp.concatenate(gain_rows, axis=0)
    mean1 = scaled_sum * (1.0 / WIDTH)
    mean2 = cross_sum * (1.0 / WIDTH)
    for b in range(4):
        cut = slice(b * 256, (b + 1) * 256)
        dhid[:, cut] = (
            dout[:, cut].astype(F32) + inv_std * (scaled_all[b] - mean1 - mixed[:, cut] * mean2)
        ).astype(BF)
    for h in range(N_SRC):
        og[h] = nt(dhid[...], w_out[h * HEAD : (h + 1) * HEAD, :]).astype(BF)
    for swap in (x_swap, g_swap, m_swap, xa_swap, ga_swap, ma_swap, p_swap, gp_swap, b_swap, gb_swap):
        swap.sent_all()


def backward_kernel(
    og, qh, kh, vh, oT, stat, len_ref, att, dhid, r_part, g_part,
    dq, dk, dv, dw, d_router, d_gain,
    ogr, dqs, dqr, dka, dva, dks, dvs, dkr, dvr, kT, bias, pbuf, dsbuf,
    w1, c1, w2, yr, w3, sr, x4, xr, rg, rsend, ra, gr, gt, gmid,
    og_sem, dq_sem, dk_sem, dv_sem, c_sem, y_sem, s_sem, xh_sem, rg_sem, ra_sem, gr_sem, gt_sem,
):
    src, tok = lax.axis_index("src"), lax.axis_index("tok")
    greet(src, tok)
    y_me, x_me, c_me = tok // 4, (tok // 2) % 2, tok % 2
    og_swap = Swap("src", src, og_sem, lambda p: og.at[p], lambda i: ogr.at[i])
    dq_swap = Swap("src", src, dq_sem, lambda p: dqs.at[p], lambda i: dqr.at[i])
    dk_swap = Swap("src", src, dk_sem, lambda p: dks.at[rows(p, 128)], lambda i: dkr.at[i])
    dv_swap = Swap("src", src, dv_sem, lambda p: dvs.at[rows(p, 128)], lambda i: dvr.at[i])
    s_swap = Swap("src", src, s_sem, lambda p: w3.at[p], lambda i: sr.at[i])
    rg_swap = Swap("src", src, rg_sem, lambda p: rg.at[src], lambda i: rg.at[i])
    ra_swap = Swap("tok", tok, ra_sem, lambda p: rsend, lambda i: ra.at[i])
    gr_swap = Swap("src", src, gr_sem, lambda p: g_part, lambda i: gr.at[i])
    gt_swap = Swap("tok", tok, gt_sem, lambda p: gmid, lambda i: gt.at[i])
    og_swap.send_all()
    gr_swap.send_all()
    gr[src] = g_part[...]
    ogr[src] = og[src]

    for i in range(8):
        cut = slice(i * HEAD, (i + 1) * HEAD)
        attT = att[:, cut].astype(F32).T.astype(BF)
        w = nn(attT, dhid[...]).astype(BF)
        w1[i, 0, :, :WIDTH] = w[:64]
        w1[i, 1, :, :WIDTH] = w[64:]
        r = r_part[cut, :].astype(BF)
        w1[i, 0, :, WIDTH:] = r[:64]
        w1[i, 1, :, WIDTH:] = r[64:]
    core_copy = remote(w1.at[:, 1 - c_me], c1, c_sem.at[0], c_sem.at[1], "tok", tok_step(tok, 1))
    core_copy.start()

    kT[...] = kh[...].astype(F32).T.astype(BF)
    fill_bias(len_ref[tok], bias)
    dka[...] = jnp.zeros_like(dka)
    dva[...] = jnp.zeros_like(dva)

    def block(b):
        q, d_o = qh[b], ogr[b]
        row_term = jnp.sum(d_o.astype(F32).T * oT[b].astype(F32), axis=0, keepdims=True)
        top, inv = stat[b][0:1, :], stat[b][8:9, :]
        for c in range(0, SRC_ALL, 128):
            s = nt(kh[c : c + 128, :], q) + bias[c : c + 128, :]
            p = jnp.exp2((s - top) * EXP2_SCALE) * inv
            pbuf[c : c + 128, :] = p.astype(BF)
            dp = nt(vh[c : c + 128, :], d_o)
            dsbuf[c : c + 128, :] = (p * (dp - row_term) * FACTOR).astype(BF)
        dqs[b] = nn(kT[...], dsbuf[...]).T.astype(BF)
        dka[...] += nn(dsbuf[...], q)
        dva[...] += nn(pbuf[...], d_o)

    def turn(k):
        og_swap.arrive(k)
        block(src_step(src, k, True))
        dq_swap.send(src_step(0, k, True))

    block(src)
    dqr[src] = dqs[src]

    core_copy.wait_recv()
    for i in range(8):
        w2[i] = (w1[i, c_me].astype(F32) + c1[i].astype(F32)).astype(BF)

    def y_copy(k, to, slot):
        return remote(w2.at[pl.ds((to // 4) * 2, 2)], yr.at[slot // 4], y_sem.at[0, k], y_sem.at[1, k], "tok", to)

    each(4, lambda k: y_copy(k, tok_step(tok, 4 * k), tok).start())
    yr[y_me] = w2[pl.ds(y_me * 2, 2)]
    for k in (1, 2, 3):
        turn(k)
    gr_swap.arrive_all()
    gmid[...] = jnp.sum(gr[...], axis=0)
    gt_swap.send_all()
    gt[tok] = gmid[...]

    def y_done(k):
        sender = tok_step(tok, 4 * k, True)
        y_copy(k, sender, sender).wait_recv()

    each(4, y_done)
    for x in range(2):
        sums = jnp.sum(yr[:, x].astype(F32), axis=0)
        x4[x] = sums
    for i in range(8):
        w3[i] = jnp.concatenate([x4[0, i * 8 : (i + 1) * 8, :], x4[1, i * 8 : (i + 1) * 8, :]], axis=0).astype(BF)
    s_swap.send_all()
    sr[src] = w3[src]
    for k in (4, 5):
        turn(k)
    s_swap.arrive_all()
    sums = jnp.sum(sr[...].astype(F32), axis=0)
    xr[0] = sums[:8]
    xr[1] = sums[8:]
    x_copy = remote(xr.at[1 - x_me], xr.at[2], xh_sem.at[0], xh_sem.at[1], "tok", tok_step(tok, 2))
    x_copy.start()
    for k in (6, 7):
        turn(k)
    dks[...] = dka[...].astype(BF)
    dk_swap.send_all()
    dvs[...] = dva[...].astype(BF)
    dv_swap.send_all()
    dkr[src] = dks[rows(src, 128), :]
    dvr[src] = dvs[rows(src, 128), :]
    x_copy.wait_recv()
    mine = xr[x_me] + xr[2]
    dw[...] = mine[:, :WIDTH]
    rg[src] = mine[:, WIDTH:]
    rg_swap.send_all()
    rg_swap.arrive_all()
    for i in range(0, 8, 2):
        rsend[i * 8 : i * 8 + 16, :] = jnp.concatenate([rg[i], rg[i + 1]], axis=0).astype(BF)
    ra_swap.send_all()
    ra[tok] = rsend[...]
    gt_swap.arrive_all()
    d_gain[...] = jnp.sum(gt[...], axis=0)
    dq_swap.arrive_all()
    for h in range(N_SRC):
        dq[:, h * HEAD : (h + 1) * HEAD] = dqr[h]
    dk_swap.arrive_all()
    dv_swap.arrive_all()
    for h in range(N_SRC):
        dk[:, h * HEAD : (h + 1) * HEAD] = dkr[h]
        dv[:, h * HEAD : (h + 1) * HEAD] = dvr[h]
    ra_swap.arrive_all()
    for t in range(N_TOK):
        d_router[t * 64 : (t + 1) * 64, :] = ra[t].astype(F32)
    for swap in (og_swap, dq_swap, dk_swap, dv_swap, s_swap, rg_swap, ra_swap, gr_swap, gt_swap):
        swap.sent_all()
    core_copy.wait_send()
    x_copy.wait_send()
    each(4, lambda k: y_copy(k, tok_step(tok, 4 * k), tok).wait_send())


VMEM = pl.BlockSpec(memory_space=pltpu.VMEM)
SMEM = pl.BlockSpec(memory_space=pltpu.SMEM)


def call(kernel, in_specs, outs, scratch, collective_id, args):
    return pl.pallas_call(
        kernel,
        out_shape=tuple(jax.ShapeDtypeStruct(s, d) for s, d in outs),
        in_specs=in_specs,
        out_specs=tuple(VMEM for _ in outs),
        scratch_shapes=scratch,
        compiler_params=pltpu.CompilerParams(
            collective_id=collective_id, has_side_effects=True, vmem_limit_bytes=58 * 1024 * 1024
        ),
    )(*args)


def vm(*shape, dtype=BF):
    return pltpu.VMEM(shape, dtype)


def sems(*shape):
    return pltpu.SemaphoreType.DMA(shape)


def on_device(
    hidden_in, d_out, queries, keys, values, source_len, out_weight, norm_gain, router,
    expert_ids, expert_slots, fc_in, fc_out,
):
    att, qh, kh, vh, oT, stat = call(
        attend_kernel,
        [VMEM, VMEM, VMEM, SMEM],
        [
            ((ROWS, WIDTH), BF), ((8, ROWS, HEAD), BF), ((SRC_ALL, HEAD), BF), ((SRC_ALL, HEAD), BF),
            ((8, HEAD, ROWS), BF), ((8, 16, ROWS), F32),
        ],
        [
            vm(8, ROWS, HEAD), vm(SRC_ALL, HEAD), vm(SRC_ALL, HEAD), vm(8, ROWS, HEAD), vm(8, ROWS, HEAD),
            vm(HEAD, SRC_ALL), vm(SRC_ALL, ROWS, dtype=F32), vm(SRC_ALL, ROWS), vm(SRC_ALL, ROWS, dtype=F32),
        ] + [sems(2, 8)] * 4,
        1,
        (queries, keys[0], values[0], source_len),
    )
    dhid, og, d_fin, d_fout, r_part, g_part = call(
        expert_kernel,
        [VMEM] * 10,
        [
            ((ROWS, WIDTH), BF), ((8, ROWS, HEAD), BF), ((512, WIDTH), BF), ((512, WIDTH), BF),
            ((WIDTH, HEAD), F32), ((8, HEAD), F32),
        ],
        [
            vm(ROWS, WIDTH, dtype=F32), vm(ROWS, WIDTH), vm(ROWS, ROWS), vm(ROWS, ROWS),
            vm(ROWS, ROWS), vm(ROWS, ROWS), vm(HEAD, HEAD, dtype=F32),
            vm(ROWS, ROWS), vm(ROWS, ROWS), vm(HEAD, HEAD, dtype=F32),
            vm(512, WIDTH), vm(512, WIDTH), vm(8, 8, HEAD, dtype=F32),
            vm(512, 512), vm(512, 512), vm(512, 512), vm(512, WIDTH), vm(8, 64, WIDTH),
            vm(4, 8, HEAD, dtype=F32), vm(8, 8, HEAD, dtype=F32),
            vm(ROWS, ROWS), vm(ROWS, ROWS), vm(8, HEAD, dtype=F32), vm(HEAD, HEAD, dtype=F32),
        ] + [sems(2, 16)] * 3 + [sems(2, 8)] * 5 + [sems(2, 16)] * 2,
        2,
        (att, hidden_in, d_out, out_weight, norm_gain[None], router, expert_ids, expert_slots, fc_in[0], fc_out[0]),
    )
    wide = WIDTH + HEAD
    dq, dk, dv, dw, d_router, d_gain = call(
        backward_kernel,
        [VMEM] * 6 + [SMEM] + [VMEM] * 4,
        [
            ((ROWS, WIDTH), BF), ((HEAD, WIDTH), BF), ((HEAD, WIDTH), BF), ((8, WIDTH), F32),
            ((WIDTH, HEAD), F32), ((8, HEAD), F32),
        ],
        [
            vm(8, ROWS, HEAD), vm(8, ROWS, HEAD), vm(8, ROWS, HEAD),
            vm(SRC_ALL, HEAD, dtype=F32), vm(SRC_ALL, HEAD, dtype=F32), vm(SRC_ALL, HEAD), vm(SRC_ALL, HEAD),
            vm(8, HEAD, HEAD), vm(8, HEAD, HEAD), vm(HEAD, SRC_ALL), vm(SRC_ALL, ROWS, dtype=F32),
            vm(SRC_ALL, ROWS), vm(SRC_ALL, ROWS),
            vm(8, 2, 64, wide), vm(8, 64, wide), vm(8, 64, wide), vm(4, 2, 64, wide), vm(8, 16, wide),
            vm(8, 16, wide), vm(2, 64, wide, dtype=F32), vm(3, 8, wide, dtype=F32),
            vm(8, 8, HEAD, dtype=F32), vm(64, HEAD), vm(16, 64, HEAD), vm(8, 8, HEAD, dtype=F32),
            vm(16, 8, HEAD, dtype=F32), vm(8, HEAD, dtype=F32),
        ] + [sems(2, 8)] * 4 + [sems(2), sems(2, 4), sems(2, 8), sems(2), sems(2, 8), sems(2, 16), sems(2, 8), sems(2, 16)],
        3,
        (og, qh, kh, vh, oT, stat, source_len, att, dhid, r_part, g_part),
    )
    return (
        dhid, dq, dk[None], dv[None], dw, d_router, d_gain.reshape(-1), d_fin[None], d_fout[None],
    )


def solution(mesh):
    return jax.shard_map(
        on_device,
        mesh=mesh,
        in_specs=(
            P(("tok", "src"), None), P(("tok", "src"), None), P(("tok", "src"), None),
            P("tok", "src", None), P("tok", "src", None), P(), P(), P(), P(),
            P(("tok", "src"), None), P(("tok", "src"), None), P("tok", "src", None), P("tok", "src", None),
        ),
        out_specs=(
            P(("tok", "src"), None), P(("tok", "src"), None), P("tok", "src", None), P("tok", "src", None),
            P(("tok", "src"), None), P(), P(), P("tok", "src", None), P("tok", "src", None),
        ),
        check_vma=False,
    )
```

```python
import math

import jax
import jax.numpy as jnp
from jax import lax
from jax.experimental import pallas as pl
from jax.experimental.pallas import tpu as pltpu
from jax.sharding import PartitionSpec as P

MESH = pl.DeviceIdType.MESH
BF, F32 = jnp.bfloat16, jnp.float32
HEAD = 128
CAP = 4
NORM_EPS = 1e-05
GELU_SCALE = 0.7978845608028654
CUBIC_TERM = 0.044715
FACTOR = 1.0 / math.sqrt(HEAD)
EXP2_SCALE = FACTOR / math.log(2.0)
MASKED = -1e30
N_SRC, N_TOK = 8, 16
ROWS, WIDTH, SRC_ALL = 256, 1024, 1024


def nn(a, b, **kw):
    return lax.dot_general(a, b, (((1,), (0,)), ((), ())), preferred_element_type=F32, **kw)


def nt(a, b, **kw):
    return lax.dot_general(a, b, (((1,), (1,)), ((), ())), preferred_element_type=F32, **kw)


def src_step(src, k, back=False):
    x, z = src // 4, src % 4
    z = (z + 4 - k % 4) % 4 if back else (z + k % 4) % 4
    return ((x + k // 4) % 2) * 4 + z


def tok_step(tok, k, back=False):
    y, x, c = tok // 4, (tok // 2) % 2, tok % 2
    y = (y + 4 - k // 4) % 4 if back else (y + k // 4) % 4
    return y * 4 + ((x + (k // 2) % 2) % 2) * 2 + (c + k % 2) % 2


def remote(src_ref, dst_ref, send_sem, recv_sem, axis, peer):
    return pltpu.make_async_remote_copy(
        src_ref=src_ref,
        dst_ref=dst_ref,
        send_sem=send_sem,
        recv_sem=recv_sem,
        device_id={axis: peer},
        device_id_type=MESH,
    )


def each(count, body, low=1):
    def step(k, carry):
        body(k)
        return carry

    lax.fori_loop(low, count, step, 0)


def greet(src, tok):
    bar = pltpu.get_barrier_semaphore()
    waits = 0
    if src is not None:
        waits += N_SRC - 1
        each(N_SRC, lambda k: pl.semaphore_signal(bar, inc=1, device_id={"src": src_step(src, k)}, device_id_type=MESH))
    if tok is not None:
        waits += N_TOK - 1
        each(N_TOK, lambda k: pl.semaphore_signal(bar, inc=1, device_id={"tok": tok_step(tok, k)}, device_id_type=MESH))
    pl.semaphore_wait(bar, waits)


class Swap:
    def __init__(self, axis, me, sems, source, target, blocks, low=1, high=None):
        self.axis, self.me, self.sems = axis, me, sems
        self.source, self.target = source, target
        self.low, self.high = low, high or (N_SRC if axis == "src" else N_TOK)
        self.held = blocks(self.high - low)
        self.step = src_step if axis == "src" else tok_step

    def send(self, k):
        to = self.step(self.me, k)
        remote(self.source(to), self.target(self.me), self.sems.at[0], self.sems.at[1], self.axis, to).start()

    def send_all(self):
        each(self.high, self.send, self.low)

    def arrive_all(self):
        bulk_wait(self.held, self.sems.at[1])

    def sent_all(self):
        bulk_wait(self.held, self.sems.at[0])


def bulk_wait(ref, sem):
    pltpu.make_async_copy(ref, ref, sem).wait()


def lanes(index):
    return pl.ds(pl.multiple_of(index * HEAD, HEAD), HEAD)


def rows(index, size):
    return pl.ds(pl.multiple_of(index * size, size), size)


def fold8(value, op):
    return op(value.reshape(value.shape[0] // 8, 8, value.shape[1]), axis=0)


def gelu_pair(x):
    k = jnp.tanh(GELU_SCALE * (x + CUBIC_TERM * x * x * x))
    value = 0.5 * x * (1.0 + k)
    slope = 0.5 * (1.0 + k) + 0.5 * x * (1.0 - k * k) * GELU_SCALE * (1.0 + 3.0 * CUBIC_TERM * x * x)
    return value, slope


def iota(shape, dim):
    return lax.broadcasted_iota(jnp.int32, shape, dim)


def vm(*shape, dtype=BF):
    return pltpu.VMEM(shape, dtype)


def sems(*shape):
    return pltpu.SemaphoreType.DMA(shape)


SCRATCH = dict(
    hid=vm(ROWS, WIDTH), w_out=vm(WIDTH, WIDTH), f_in=vm(512, WIDTH), f_out=vm(512, WIDTH),
    qh=vm(8, ROWS, HEAD), kh=vm(SRC_ALL, HEAD), vh=vm(SRC_ALL, HEAD), att_in=vm(8, ROWS, HEAD),
    att_send=vm(8, ROWS, HEAD), vT=vm(HEAD + 16, SRC_ALL), kT=vm(HEAD, SRC_ALL), sbuf=vm(SRC_ALL, ROWS, dtype=F32),
    pbuf=vm(SRC_ALL, ROWS), dsbuf=vm(SRC_ALL, ROWS),
    oT=vm(8, HEAD, ROWS), stat=vm(8, 16, ROWS, dtype=F32), att=vm(ROWS, WIDTH),
    mixed=vm(ROWS, WIDTH, dtype=F32), xin=vm(ROWS, WIDTH), hitT=vm(ROWS, ROWS),
    xs=vm(ROWS, ROWS), gs=vm(ROWS, ROWS), ms=vm(HEAD, HEAD, dtype=F32),
    xr=vm(ROWS, ROWS), gr=vm(ROWS, ROWS), mr=vm(HEAD, HEAD, dtype=F32),
    xall=vm(512, WIDTH), gall=vm(512, WIDTH), mall=vm(8, 8, HEAD, dtype=F32),
    backT=vm(512, 512, dtype=F32), actg=vm(512, 512), dpT=vm(512, 512), dpr=vm(512, 512),
    part=vm(512, WIDTH), pr=vm(8, 64, WIDTH), gps=vm(4, 8, HEAD, dtype=F32), gpr=vm(8, 8, HEAD, dtype=F32),
    ps=vm(ROWS, ROWS), br=vm(ROWS, ROWS), gsum=vm(8, HEAD, dtype=F32), gb=vm(HEAD, HEAD, dtype=F32),
    dhid=vm(ROWS, WIDTH), d_fin=vm(512, WIDTH), d_fout=vm(512, WIDTH),
    og=vm(8, ROWS, HEAD), ogr=vm(8, ROWS, HEAD), dqs=vm(8, ROWS, HEAD), dqr=vm(8, ROWS, HEAD),
    dka=vm(SRC_ALL, HEAD, dtype=F32), dva=vm(SRC_ALL, HEAD, dtype=F32), dks=vm(SRC_ALL, HEAD), dvs=vm(SRC_ALL, HEAD),
    dkr=vm(8, HEAD, HEAD), dvr=vm(8, HEAD, HEAD),
    w1=vm(8, 2, 64, WIDTH), c1=vm(8, 64, WIDTH), x5=vm(3, 8, WIDTH, dtype=F32),
    wtmp=vm(8, 64, 512, dtype=F32), ya=vm(8, 64, 512), yar=vm(4, 2, 64, 512), sa=vm(8, 16, 512), sar=vm(8, 16, 512),
    sb=vm(8, 64, 512), sbr=vm(8, 64, 512), yb=vm(4, 16, 512), ybr=vm(4, 16, 512),
    r1=vm(16, 64, HEAD), r1r=vm(16, 64, HEAD), r2=vm(8, 64, HEAD), r3=vm(16, 64, HEAD),
    g1=vm(8, 8, HEAD, dtype=F32), g2=vm(16, 8, HEAD, dtype=F32),
    dw=vm(8, WIDTH, dtype=F32), d_router=vm(WIDTH, HEAD, dtype=F32), d_gain=vm(8, HEAD, dtype=F32),
    dout=vm(ROWS, WIDTH),
    k_sem=sems(2), v_sem=sems(2), qn_sem=sems(2), qf_sem=sems(2), a_sem=sems(2), x_sem=sems(2), g_sem=sems(2),
    m_sem=sems(2), xan_sem=sems(2), xaf_sem=sems(2), ga_sem=sems(2), ma_sem=sems(2), p_sem=sems(2),
    gp_sem=sems(2), b_sem=sems(2), gb_sem=sems(2), ogn_sem=sems(2), ogf_sem=sems(2), dq_sem=sems(2),
    dk_sem=sems(2), dv_sem=sems(2), c_sem=sems(2), xh_sem=sems(2), ya_sem=sems(2), yb_sem=sems(2), sa_sem=sems(2),
    sb_sem=sems(2), r1_sem=sems(2), r2_sem=sems(2), r3_sem=sems(2), g1_sem=sems(2), g2_sem=sems(2),
    io_sem=sems(17),
)
INPUTS = (
    "length", "gain", "router", "ids", "slots", "q", "k", "v", "dout_hbm", "hid_hbm", "w_out_hbm",
    "f_in_hbm", "f_out_hbm",
)
OUTPUTS = (
    "dhid_hbm", "dq_hbm", "dk_hbm", "dv_hbm", "dw_hbm", "d_router_hbm", "d_gain_hbm", "d_fin_hbm",
    "d_fout_hbm",
)


class Refs:
    pass


def block_kernel(*refs):
    R = Refs()
    for name, ref in zip(INPUTS + OUTPUTS + tuple(SCRATCH), refs, strict=True):
        setattr(R, name, ref)
    src, tok = lax.axis_index("src"), lax.axis_index("tok")
    y_me, x_me, c_me = tok // 4, (tok // 2) % 2, tok % 2
    x_lo = src // 4

    loads = [
        pltpu.make_async_copy(a, b, R.io_sem.at[i])
        for i, (a, b) in enumerate(
            (
                (R.dout_hbm, R.dout), (R.hid_hbm, R.hid), (R.w_out_hbm, R.w_out), (R.f_out_hbm, R.f_out), (R.f_in_hbm, R.f_in),
                (R.k.at[:, lanes(src)], R.kh.at[rows(src, 128)]), (R.v.at[:, lanes(src)], R.vh.at[rows(src, 128)]),
                (R.q.at[:, lanes(src)], R.qh.at[src]),
            )
        )
    ]
    for copy in loads:
        copy.start()
    greet(src, tok)

    def by_src(*way):
        return Swap("src", src, *way)

    def by_tok(*way):
        return Swap("tok", tok, *way)

    def first(ref, size=1):
        return lambda n: ref.at[pl.ds(0, n * size)]

    def at(ref):
        return lambda i: ref.at[i]

    def at_rows(ref, size):
        return lambda i: ref.at[rows(i, size)]

    k_swap = by_src(R.k_sem, lambda p: R.k.at[:, lanes(p)], at_rows(R.kh, 128), first(R.kh, 128))
    v_swap = by_src(R.v_sem, lambda p: R.v.at[:, lanes(p)], at_rows(R.vh, 128), first(R.vh, 128))
    q_way = lambda p: R.q.at[:, lanes(p)], at(R.qh), first(R.qh)
    q_near, q_far = by_src(R.qn_sem, *q_way, 1, 4), by_src(R.qf_sem, *q_way, 4, 8)
    a_swap = by_src(R.a_sem, at(R.att_send), at(R.att_in), first(R.att_in))
    x_swap = by_tok(R.x_sem, at_rows(R.xs, 16), at_rows(R.xr, 16), first(R.xr, 16))
    g_swap = by_tok(R.g_sem, at_rows(R.gs, 16), at_rows(R.gr, 16), first(R.gr, 16))
    m_swap = by_tok(R.m_sem, at_rows(R.ms, 8), at_rows(R.mr, 8), first(R.mr, 8))
    xa_way = lambda p: R.xall.at[rows(src, 64)], at_rows(R.xall, 64), first(R.xall, 64)
    xa_near, xa_far = by_src(R.xan_sem, *xa_way, 1, 4), by_src(R.xaf_sem, *xa_way, 4, 8)
    ga_swap = by_src(R.ga_sem, lambda p: R.gall.at[rows(src, 64)], at_rows(R.gall, 64), first(R.gall, 64))
    ma_swap = by_src(R.ma_sem, lambda p: R.mall.at[src], at(R.mall), first(R.mall))
    p_swap = by_src(R.p_sem, at_rows(R.part, 64), at(R.pr), first(R.pr))
    gp_swap = by_src(R.gp_sem, lambda p: R.gps.at[p // 2], at(R.gpr), first(R.gpr))
    b_swap = by_tok(R.b_sem, at_rows(R.ps, 16), at_rows(R.br, 16), first(R.br, 16))
    gb_swap = by_tok(R.gb_sem, lambda p: R.gsum, at_rows(R.gb, 8), first(R.gb, 8))
    og_way = at(R.og), at(R.ogr), first(R.ogr)
    og_near, og_far = by_src(R.ogn_sem, *og_way, 1, 4), by_src(R.ogf_sem, *og_way, 4, 8)
    dq_swap = by_src(R.dq_sem, at(R.dqs), at(R.dqr), first(R.dqr))
    dk_swap = by_src(R.dk_sem, at_rows(R.dks, 128), at(R.dkr), first(R.dkr))
    dv_swap = by_src(R.dv_sem, at_rows(R.dvs, 128), at(R.dvr), first(R.dvr))
    sa_swap = by_src(R.sa_sem, at(R.sa), at(R.sar), first(R.sar))
    sb_swap = by_src(R.sb_sem, at(R.sb), at(R.sbr), first(R.sbr))
    r1_swap = by_tok(R.r1_sem, at(R.r1), at(R.r1r), first(R.r1r))
    r2_swap = by_src(R.r2_sem, lambda p: R.r2.at[src], at(R.r2), first(R.r2))
    r3_swap = by_tok(R.r3_sem, lambda p: R.r3.at[tok], at(R.r3), first(R.r3))
    g1_swap = by_src(R.g1_sem, lambda p: R.g1.at[src], at(R.g1), first(R.g1))
    g2_swap = by_tok(R.g2_sem, lambda p: R.g2.at[tok], at(R.g2), first(R.g2))

    def y_go(sem, source, target, held):
        def send(k):
            to = tok_step(tok, 4 * k)
            remote(source(to // 4), target(y_me), sem.at[0], sem.at[1], "tok", to).start()

        each(4, send)

    def y_arrive(sem, source, target, held):
        bulk_wait(held, sem.at[1])

    def y_sent(sem, source, target, held):
        bulk_wait(held, sem.at[0])

    ya_way = (R.ya_sem, lambda y: R.ya.at[pl.ds(y * 2, 2)], at(R.yar), R.yar.at[pl.ds(0, 3)])
    yb_way = (R.yb_sem, at(R.yb), at(R.ybr), R.ybr.at[pl.ds(0, 3)])

    k_swap.send_all()
    v_swap.send_all()

    def aim_of(id_of, slot_of):
        return jnp.where((id_of < N_TOK) & (slot_of >= 0), id_of * CAP + slot_of, -1)

    j = iota((ROWS, ROWS), 0)
    key = (j // 16) * CAP + j % CAP
    aim_rows = aim_of(R.ids[...], R.slots[...])
    hitT = jnp.where((aim_rows[0:1, :] == key) | (aim_rows[1:2, :] == key), 1.0, 0.0)
    R.hitT[...] = hitT.astype(BF)
    row_blk = (j // CAP) % 4
    zero = jnp.zeros((ROWS, ROWS), BF)

    def to_experts(ref, out):
        acc = None
        for b in range(4):
            term = nn(jnp.where(row_blk == b, R.hitT[...], zero), ref[:, b * 256 : (b + 1) * 256])
            acc = term if acc is None else acc + term
        out[...] = acc.astype(BF)

    loads[0].wait()
    to_experts(R.dout, R.gs)
    g_swap.send_all()
    k_swap.sent_all()
    v_swap.sent_all()
    q_near.send_all()
    q_near.sent_all()
    q_far.send_all()
    R.gr[rows(tok, 16), :] = R.gs[rows(tok, 16), :]
    for copy in loads[5:]:
        copy.wait()
    k_swap.arrive_all()
    v_swap.arrive_all()
    length = R.length[tok]
    seen = iota((SRC_ALL, HEAD), 0) < length
    seen_row = iota((HEAD, SRC_ALL), 1) < length
    k_wide = R.kh[...].astype(F32)
    R.kh[...] = jnp.where(seen, k_wide, k_wide[0:1, :]).astype(BF)
    R.vT[:HEAD, :] = jnp.where(seen_row, R.vh[...].astype(F32).T, 0.0).astype(BF)
    R.vT[HEAD:, :] = jnp.where(seen_row[:16], 1.0, 0.0).astype(BF)

    def forward_block(b):
        q = R.qh[b]
        top = jnp.full((8, ROWS), -3e38, F32)
        for c in range(0, SRC_ALL, 128):
            s = nt(R.kh[c : c + 128, :], q)
            R.sbuf[c : c + 128, :] = s
            top = jnp.maximum(top, fold8(s, jnp.max))
        top = jnp.max(top, axis=0, keepdims=True)
        for c in range(0, SRC_ALL, 128):
            p = jnp.exp2((R.sbuf[c : c + 128, :] - top) * EXP2_SCALE)
            R.pbuf[c : c + 128, :] = p.astype(BF)
        summed = nn(R.vT[...], R.pbuf[...])
        inv = 1.0 / summed[HEAD : HEAD + 1, :]
        oT = summed[:HEAD, :] * inv
        R.oT[b] = oT.astype(BF)
        R.stat[b] = jnp.concatenate(
            [jnp.broadcast_to(top, (8, ROWS)), jnp.broadcast_to(inv, (8, ROWS))], axis=0
        )
        R.att_send[b] = oT.T.astype(BF)

    i64, j256 = iota((64, ROWS), 0), iota((64, ROWS), 1)
    take = [jnp.where(j256 == (i64 // CAP) * 16 + b * CAP + i64 % CAP, 1.0, 0.0).astype(BF) for b in range(4)]

    def unpack(got, out):
        for b in range(4):
            out[rows(src, 64), b * 256 : (b + 1) * 256] = nn(take[b], got[...]).astype(BF)

    def g_on():
        g_swap.arrive_all()
        unpack(R.gr, R.gall)
        ga_swap.send_all()

    forward_block(src)
    R.att_in[src] = R.att_send[src]

    def forward_turn(k):
        forward_block(src_step(src, k, True))
        a_swap.send(src_step(0, k, True))

    q_near.arrive_all()
    each(4, forward_turn)
    q_far.arrive_all()
    each(8, forward_turn, 4)

    id_cols = jnp.concatenate([R.ids[...], R.slots[...], R.ids[...], R.slots[...]], axis=0).astype(F32).T
    id_cols = id_cols.astype(jnp.int32)
    id1, id2, slot1, slot2 = (id_cols[:, i : i + 1] for i in range(4))
    lane = iota((ROWS, HEAD), 1)
    pick1 = jnp.where(id1 == lane, 1.0, 0.0)
    pick2 = jnp.where(id2 == lane, 1.0, 0.0)
    live1, live2 = slot1 >= 0, slot2 >= 0
    base = (src % 2) * 64 + tok * CAP
    own1 = jnp.where(live1 & (id1 < N_TOK) & (id1 == lane // 8), 1.0, 0.0)
    own2 = jnp.where(live2 & (id2 < N_TOK) & (id2 == lane // 8), 1.0, 0.0)
    at1 = jnp.where(live1 & (lane == base + slot1), 1.0, 0.0)
    at2 = jnp.where(live2 & (lane == base + slot2), 1.0, 0.0)
    for copy in loads[1:5]:
        copy.wait()
    a_swap.arrive_all()
    for h in range(N_SRC):
        R.att[:, h * HEAD : (h + 1) * HEAD] = R.att_in[h]

    R.mixed[...] = R.hid[...].astype(F32) + nn(R.att[...], R.w_out[...])
    inv_parts = []
    for r in range(0, ROWS, 64):
        m = R.mixed[r : r + 64, :]
        centred = m - jnp.mean(m, axis=1, keepdims=True)
        inv = lax.rsqrt(jnp.mean(centred * centred, axis=1, keepdims=True) + NORM_EPS)
        inv_parts.append(inv)
        normed = centred * inv
        R.mixed[r : r + 64, :] = normed
        R.xin[r : r + 64, :] = (normed * R.gain[...]).astype(BF)
    inv_std = jnp.concatenate(inv_parts, axis=0)
    to_experts(R.xin, R.xs)
    x_swap.send_all()
    g_on()
    R.xr[rows(tok, 16), :] = R.xs[rows(tok, 16), :]
    logits = nn(R.xin[...], R.router[...])
    gap = jnp.sum(logits * (pick1 - pick2), axis=1, keepdims=True)
    gate1 = 1.0 / (1.0 + jnp.exp(-gap))
    gate2 = 1.0 / (1.0 + jnp.exp(gap))
    low1 = gate1.astype(BF).astype(F32)
    low2 = gate2.astype(BF).astype(F32)
    R.ms[...] = nn((own1 * low1).T.astype(BF), at1.astype(BF)) + nn((own2 * low2).T.astype(BF), at2.astype(BF))
    m_swap.send_all()
    R.mr[rows(tok, 8), :] = R.ms[rows(tok, 8), :]
    for swap in (q_far, a_swap, g_swap):
        swap.sent_all()

    x_swap.arrive_all()
    unpack(R.xr, R.xall)
    xa_near.send_all()
    xa_far.send_all()
    m_swap.arrive_all()
    R.mall[src] = fold8(R.mr[...], jnp.sum)
    ma_swap.send_all()
    ga_swap.arrive_all()
    for c in range(0, 512, 128):
        R.backT[c : c + 128, :] = nt(R.f_out[c : c + 128, :], R.gall[...])
    R.kT[...] = jnp.where(seen_row, R.kh[...].astype(F32).T, 0.0).astype(BF)
    for swap in (x_swap, m_swap, ga_swap):
        swap.sent_all()
    ma_swap.arrive_all()

    for half, steps, xa_swap in ((x_lo, (1, 4), xa_near), (1 - x_lo, (4, 8), xa_far)):
        xa_swap.arrive_all()
        here = rows(half, 256)
        x_half = R.xall[here, :]
        m4 = half * 4
        gate_row = jnp.concatenate(
            [R.mall[m4][0:1, :] + R.mall[m4 + 1][0:1, :], R.mall[m4 + 2][0:1, :] + R.mall[m4 + 3][0:1, :]], axis=1
        )
        gate_acc = jnp.zeros((8, 256), F32)
        for c in range(0, 512, 128):
            value, slope = gelu_pair(nt(R.f_in[c : c + 128, :], x_half))
            act = value.astype(BF).astype(F32)
            back = R.backT[c : c + 128, here]
            gate_acc = gate_acc + fold8(back * act, jnp.sum)
            R.actg[c : c + 128, here] = (act * gate_row).astype(BF)
            dp = gate_row * back * slope
            R.dpT[c : c + 128, here] = dp.astype(BF)
            R.dpr[here, c : c + 128] = dp.T.astype(BF)
        gate_tot = jnp.sum(gate_acc, axis=0, keepdims=True)
        R.gps[half * 2] = jnp.broadcast_to(gate_tot[:, :HEAD], (8, HEAD))
        R.gps[half * 2 + 1] = jnp.broadcast_to(gate_tot[:, HEAD:], (8, HEAD))
        R.part[here, :] = nn(R.dpr[here, :], R.f_in[...]).astype(BF)
        each(steps[1], p_swap.send, steps[0])
        each(steps[1], gp_swap.send, steps[0])
    R.pr[src] = R.part[rows(src, 64), :]
    R.gpr[src] = R.gps[src // 2]
    stores = [
        pltpu.make_async_copy(a, b, R.io_sem.at[8 + i])
        for i, (a, b) in enumerate(
            (
                (R.d_fin, R.d_fin_hbm), (R.d_fout, R.d_fout_hbm), (R.dhid, R.dhid_hbm),
                (R.dw, R.dw_hbm), (R.d_router, R.d_router_hbm), (R.d_gain, R.d_gain_hbm),
            )
        )
    ]
    for c in range(0, 512, 128):
        R.d_fin[c : c + 128, :] = nn(R.dpT[c : c + 128, :], R.xall[...]).astype(BF)
        R.d_fout[c : c + 128, :] = nn(R.actg[c : c + 128, :], R.gall[...]).astype(BF)
    stores[0].start()
    stores[1].start()
    for swap in (xa_near, xa_far, ma_swap):
        swap.sent_all()
    gp_swap.arrive_all()
    R.gsum[...] = jnp.sum(R.gpr[...], axis=0)
    gb_swap.send_all()
    R.gb[rows(tok, 8), :] = R.gsum[...]
    p_swap.arrive_all()
    acc = None
    for b in range(4):
        blk = jnp.sum(R.pr[:, :, b * 256 : (b + 1) * 256].astype(F32), axis=0).astype(BF)
        term = nn(take[b].astype(F32).T.astype(BF), blk)
        acc = term if acc is None else acc + term
    R.ps[...] = acc.astype(BF)
    b_swap.send_all()
    R.br[rows(tok, 16), :] = R.ps[rows(tok, 16), :]

    gb_swap.arrive_all()
    first = jnp.where(lane % 8 == 0, 1.0, 0.0)
    got1 = nn(own1 * first, R.gb[...], precision=lax.Precision.HIGHEST)
    got2 = nn(own2 * first, R.gb[...], precision=lax.Precision.HIGHEST)
    grad1 = jnp.sum(got1 * at1, axis=1, keepdims=True)
    grad2 = jnp.sum(got2 * at2, axis=1, keepdims=True)
    logit_grad = gate1 * gate2 * (grad1 - grad2)
    column = (pick1 - pick2) * logit_grad
    col_hi = column.astype(BF)
    col_lo = (column - col_hi.astype(F32)).astype(BF)
    colT = column.T
    colT_hi = colT.astype(BF)
    colT_lo = (colT - colT_hi.astype(F32)).astype(BF)
    router_part = (nn(colT_hi, R.xin[...]) + nn(colT_lo, R.xin[...])).T.astype(BF)
    for t in range(N_TOK):
        R.r1[t] = router_part[t * 64 : (t + 1) * 64, :]
    r1_swap.send_all()
    R.r1r[tok] = R.r1[tok]
    for swap in (p_swap, gp_swap, gb_swap):
        swap.sent_all()
    b_swap.arrive_all()

    scaled_sum = jnp.zeros((ROWS, 1), F32)
    cross_sum = jnp.zeros((ROWS, 1), F32)
    scaled_all = []
    gain_rows = []
    for b in range(4):
        cut = slice(b * 256, (b + 1) * 256)
        mine = jnp.where(row_blk == b, R.hitT[...], zero)
        total = lax.dot_general(mine, R.br[...], (((0,), (0,)), ((), ())), preferred_element_type=F32)
        total = total + nt(col_hi, R.router[cut, :]) + nt(col_lo, R.router[cut, :])
        normed = R.mixed[:, cut]
        row = jnp.sum(total * normed, axis=0, keepdims=True)
        gain_rows += [row[:, :HEAD], row[:, HEAD:]]
        scaled = total * R.gain[:, cut]
        scaled_all.append(scaled)
        scaled_sum = scaled_sum + jnp.sum(scaled, axis=1, keepdims=True)
        cross_sum = cross_sum + jnp.sum(scaled * normed, axis=1, keepdims=True)
    mean1 = scaled_sum * (1.0 / WIDTH)
    mean2 = cross_sum * (1.0 / WIDTH)
    for b in range(4):
        cut = slice(b * 256, (b + 1) * 256)
        R.dhid[:, cut] = (
            R.dout[:, cut].astype(F32) + inv_std * (scaled_all[b] - mean1 - R.mixed[:, cut] * mean2)
        ).astype(BF)
    for h in range(N_SRC):
        R.og[h] = nt(R.dhid[...], R.w_out[h * HEAD : (h + 1) * HEAD, :]).astype(BF)
    og_near.send_all()
    og_far.send_all()
    R.g1[src] = jnp.concatenate(gain_rows, axis=0)
    g1_swap.send_all()
    stores[2].start()
    R.ogr[src] = R.og[src]

    for i in range(8):
        cut = slice(i * HEAD, (i + 1) * HEAD)
        w = nn(R.att[:, cut].astype(F32).T.astype(BF), R.dhid[...]).astype(BF)
        R.w1[i, 0] = w[:64]
        R.w1[i, 1] = w[64:]
    core_copy = remote(R.w1.at[:, 1 - c_me], R.c1, R.c_sem.at[0], R.c_sem.at[1], "tok", tok_step(tok, 1))
    core_copy.start()
    R.dka[...] = jnp.zeros_like(R.dka)
    R.dva[...] = jnp.zeros_like(R.dva)

    def backward_block(b):
        q, d_o = R.qh[b], R.ogr[b]
        d_wide = d_o.astype(F32)
        row_term = jnp.sum(d_wide.T * R.oT[b].astype(F32), axis=0, keepdims=True)
        top, inv = R.stat[b][0:1, :], R.stat[b][8:9, :]
        factor = inv * FACTOR
        scaled_d = (d_wide * R.stat[b][8:, :].T[:, 0:1]).astype(BF)
        for c in range(0, SRC_ALL, 128):
            s = nt(R.kh[c : c + 128, :], q)
            p = jnp.exp2((s - top) * EXP2_SCALE)
            R.pbuf[c : c + 128, :] = p.astype(BF)
            dp = nt(R.vh[c : c + 128, :], d_o)
            R.dsbuf[c : c + 128, :] = (p * ((dp - row_term) * factor)).astype(BF)
        R.dqs[b] = nn(R.kT[...], R.dsbuf[...]).T.astype(BF)
        R.dka[...] += nn(R.dsbuf[...], q)
        R.dva[...] += nn(R.pbuf[...], scaled_d)

    def backward_turn(k):
        backward_block(src_step(src, k, True))
        dq_swap.send(src_step(0, k, True))

    def turns(low, high):
        def step(k, carry):
            backward_turn(k)
            return carry

        lax.fori_loop(low, high, step, 0)

    backward_block(src)
    R.dqr[src] = R.dqs[src]
    core_copy.wait_recv()
    for i in range(8):
        piece = R.w1[i, c_me].astype(F32) + R.c1[i].astype(F32)
        R.ya[i] = piece[:, :512].astype(BF)
        R.wtmp[i] = piece[:, 512:]
    y_go(*ya_way)
    for s in range(N_SRC):
        R.sb[s] = jnp.concatenate([R.wtmp[i, s * 8 : (s + 1) * 8, :] for i in range(8)], axis=0).astype(BF)
    sb_swap.send_all()
    R.yar[y_me] = R.ya[pl.ds(y_me * 2, 2)]
    R.sbr[src] = R.sb[src]
    r1_swap.arrive_all()
    R.r2[src] = jnp.sum(R.r1r[...].astype(F32), axis=0).astype(BF)
    r2_swap.send_all()
    og_near.arrive_all()
    turns(1, 4)
    g1_swap.arrive_all()
    R.g2[tok] = jnp.sum(R.g1[...], axis=0)
    g2_swap.send_all()
    og_far.arrive_all()
    turns(4, 6)
    y_arrive(*ya_way)
    a0 = jnp.sum(R.yar[:, 0].astype(F32), axis=0)
    a1 = jnp.sum(R.yar[:, 1].astype(F32), axis=0)
    for s in range(N_SRC):
        R.sa[s] = jnp.concatenate([a0[s * 8 : (s + 1) * 8, :], a1[s * 8 : (s + 1) * 8, :]], axis=0).astype(BF)
    sa_swap.send_all()
    R.sar[src] = R.sa[src]
    sb_swap.arrive_all()
    sums = jnp.sum(R.sbr[...].astype(F32), axis=0)
    for y in range(4):
        R.yb[y] = sums[y * 16 : (y + 1) * 16, :].astype(BF)
    y_go(*yb_way)
    R.ybr[y_me] = R.yb[y_me]
    r2_swap.arrive_all()
    R.r3[tok] = jnp.sum(R.r2[...].astype(F32), axis=0).astype(BF)
    r3_swap.send_all()
    turns(6, 8)
    R.dks[...] = jnp.where(seen, R.dka[...], 0.0).astype(BF)
    dk_swap.send_all()
    R.dvs[...] = jnp.where(seen, R.dva[...], 0.0).astype(BF)
    dv_swap.send_all()
    R.dkr[src] = R.dks[rows(src, 128), :]
    R.dvr[src] = R.dvs[rows(src, 128), :]
    sa_swap.arrive_all()
    y_arrive(*yb_way)
    sums_a = jnp.sum(R.sar[...].astype(F32), axis=0)
    sums_b = jnp.sum(R.ybr[...].astype(F32), axis=0)
    for x in range(2):
        R.x5[x, :, :512] = sums_a[x * 8 : (x + 1) * 8, :]
        R.x5[x, :, 512:] = sums_b[x * 8 : (x + 1) * 8, :]
    x_copy = remote(R.x5.at[1 - x_me], R.x5.at[2], R.xh_sem.at[0], R.xh_sem.at[1], "tok", tok_step(tok, 2))
    x_copy.start()
    for swap in (b_swap, r1_swap, og_near, og_far, r2_swap, g1_swap, sb_swap, sa_swap):
        swap.sent_all()
    core_copy.wait_send()
    y_sent(*ya_way)
    y_sent(*yb_way)

    def keep(swap, held, out, sem):
        swap.arrive_all()
        for h in range(N_SRC):
            pltpu.make_async_copy(held.at[h], out.at[:, pl.ds(h * HEAD, HEAD)], sem).start()

    keep(dq_swap, R.dqr, R.dq_hbm, R.io_sem.at[14])
    g2_swap.arrive_all()
    R.d_gain[...] = jnp.sum(R.g2[...], axis=0)
    r3_swap.arrive_all()
    for t in range(N_TOK):
        R.d_router[t * 64 : (t + 1) * 64, :] = R.r3[t].astype(F32)
    stores[4].start()
    stores[5].start()
    x_copy.wait_recv()
    R.dw[...] = R.x5[x_me] + R.x5[2]
    stores[3].start()
    keep(dk_swap, R.dkr, R.dk_hbm, R.io_sem.at[15])
    keep(dv_swap, R.dvr, R.dv_hbm, R.io_sem.at[16])
    for swap in (r3_swap, g2_swap, dq_swap, dk_swap, dv_swap):
        swap.sent_all()
    x_copy.wait_send()
    bulk_wait(R.dqr, R.io_sem.at[14])
    bulk_wait(R.dkr, R.io_sem.at[15])
    bulk_wait(R.dvr, R.io_sem.at[16])
    for copy in stores:
        copy.wait()


def hand_over_kernel(*refs):
    count = (len(refs) - 1) // 3
    given, out, held, sem = refs[:count], refs[count : 2 * count], refs[2 * count : 3 * count], refs[-1]
    loads = [pltpu.make_async_copy(given[i], held[i], sem.at[0, i]) for i in range(count)]
    stores = [pltpu.make_async_copy(held[i], out[i], sem.at[1, i]) for i in range(count)]
    for copy in loads:
        copy.start()
    for load, store in zip(loads, stores):
        load.wait()
        store.start()
    for copy in stores:
        copy.wait()


VMEM = pl.BlockSpec(memory_space=pltpu.VMEM)
SMEM = pl.BlockSpec(memory_space=pltpu.SMEM)
HBM = pl.BlockSpec(memory_space=pl.ANY)


def on_device(
    hidden_in, d_out, queries, keys, values, source_len, out_weight, norm_gain, router,
    expert_ids, expert_slots, fc_in, fc_out,
):
    shapes = tuple(
        jax.ShapeDtypeStruct(s, d)
        for s, d in (
            ((ROWS, WIDTH), BF), ((ROWS, WIDTH), BF), ((HEAD, WIDTH), BF), ((HEAD, WIDTH), BF), ((8, WIDTH), F32),
            ((WIDTH, HEAD), F32), ((8, HEAD), F32), ((512, WIDTH), BF), ((512, WIDTH), BF),
        )
    )
    outs = pl.pallas_call(
        block_kernel,
        out_shape=shapes,
        in_specs=[SMEM] + [VMEM] * 4 + [HBM] * 8,
        out_specs=(HBM,) * 9,
        scratch_shapes=list(SCRATCH.values()),
        compiler_params=pltpu.CompilerParams(
            collective_id=1, has_side_effects=True, vmem_limit_bytes=58 * 1024 * 1024
        ),
    )(
        source_len, norm_gain[None], router, expert_ids.T, expert_slots.T, queries, keys[0], values[0], d_out,
        hidden_in, out_weight, fc_in[0], fc_out[0],
    )
    dhid, dq, dk, dv, dw, d_router, d_gain, d_fin, d_fout = pl.pallas_call(
        hand_over_kernel,
        out_shape=shapes,
        in_specs=[HBM] * 9,
        out_specs=(HBM,) * 9,
        scratch_shapes=[pltpu.VMEM(s.shape, s.dtype) for s in shapes] + [sems(2, 9)],
        compiler_params=pltpu.CompilerParams(vmem_limit_bytes=58 * 1024 * 1024),
    )(*outs)
    return dhid, dq, dk[None], dv[None], dw, d_router, d_gain.reshape(-1), d_fin[None], d_fout[None]


def solution(mesh):
    return jax.shard_map(
        on_device,
        mesh=mesh,
        in_specs=(
            P(("tok", "src"), None), P(("tok", "src"), None), P(("tok", "src"), None),
            P("tok", "src", None), P("tok", "src", None), P(), P(), P(), P(),
            P(("tok", "src"), None), P(("tok", "src"), None), P("tok", "src", None), P("tok", "src", None),
        ),
        out_specs=(
            P(("tok", "src"), None), P(("tok", "src"), None), P("tok", "src", None), P("tok", "src", None),
            P(("tok", "src"), None), P(), P(), P("tok", "src", None), P("tok", "src", None),
        ),
        check_vma=False,
    )
```

```python
import math

import jax
import jax.numpy as jnp
from jax import lax
from jax.experimental import pallas as pl
from jax.experimental.pallas import tpu as pltpu
from jax.sharding import PartitionSpec as P

MESH = pl.DeviceIdType.MESH
BF, F32 = jnp.bfloat16, jnp.float32
HEAD = 128
CAP = 4
NORM_EPS = 1e-05
GELU_SCALE = 0.7978845608028654
CUBIC_TERM = 0.044715
FACTOR = 1.0 / math.sqrt(HEAD)
EXP2_SCALE = FACTOR / math.log(2.0)
MASKED = -1e30
N_SRC, N_TOK = 8, 16
ROWS, WIDTH, SRC_ALL = 256, 1024, 1024


def nn(a, b, **kw):
    return lax.dot_general(a, b, (((1,), (0,)), ((), ())), preferred_element_type=F32, **kw)


def nt(a, b, **kw):
    return lax.dot_general(a, b, (((1,), (1,)), ((), ())), preferred_element_type=F32, **kw)


def src_step(src, k, back=False):
    x, z = src // 4, src % 4
    z = (z + 4 - k % 4) % 4 if back else (z + k % 4) % 4
    return ((x + k // 4) % 2) * 4 + z


def tok_step(tok, k, back=False):
    y, x, c = tok // 4, (tok // 2) % 2, tok % 2
    y = (y + 4 - k // 4) % 4 if back else (y + k // 4) % 4
    return y * 4 + ((x + (k // 2) % 2) % 2) * 2 + (c + k % 2) % 2


def remote(src_ref, dst_ref, send_sem, recv_sem, axis, peer):
    return pltpu.make_async_remote_copy(
        src_ref=src_ref,
        dst_ref=dst_ref,
        send_sem=send_sem,
        recv_sem=recv_sem,
        device_id={axis: peer},
        device_id_type=MESH,
    )


def each(count, body, low=1):
    def step(k, carry):
        body(k)
        return carry

    lax.fori_loop(low, count, step, 0)


def greet(src, tok):
    bar = pltpu.get_barrier_semaphore()
    waits = 0
    if src is not None:
        waits += N_SRC - 1
        each(N_SRC, lambda k: pl.semaphore_signal(bar, inc=1, device_id={"src": src_step(src, k)}, device_id_type=MESH))
    if tok is not None:
        waits += N_TOK - 1
        each(N_TOK, lambda k: pl.semaphore_signal(bar, inc=1, device_id={"tok": tok_step(tok, k)}, device_id_type=MESH))
    pl.semaphore_wait(bar, waits)


class Swap:
    def __init__(self, axis, me, sems, source, target, blocks, low=1, high=None, pick=None):
        self.pick = pick or (lambda i: i)
        self.axis, self.me, self.sems = axis, me, sems
        self.source, self.target = source, target
        self.low, self.high = low, high or (N_SRC if axis == "src" else N_TOK)
        self.held = blocks(self.high - low)
        self.step = src_step if axis == "src" else tok_step

    def send(self, k):
        to = self.step(self.me, self.pick(k))
        remote(self.source(to), self.target(self.me), self.sems.at[0], self.sems.at[1], self.axis, to).start()

    def send_all(self):
        each(self.high, self.send, self.low)

    def arrive_all(self):
        bulk_wait(self.held, self.sems.at[1])

    def sent_all(self):
        bulk_wait(self.held, self.sems.at[0])


def near_step(i):
    return 2 * i - 1 - (i - 1) // 2


def far_step(i):
    return i - 2 + 2 * ((i - 2) // 3)


def bulk_wait(ref, sem):
    pltpu.make_async_copy(ref, ref, sem).wait()


def lanes(index):
    return pl.ds(pl.multiple_of(index * HEAD, HEAD), HEAD)


def rows(index, size):
    return pl.ds(pl.multiple_of(index * size, size), size)


def fold8(value, op):
    return op(value.reshape(value.shape[0] // 8, 8, value.shape[1]), axis=0)


def gelu_pair(x):
    k = jnp.tanh(GELU_SCALE * (x + CUBIC_TERM * x * x * x))
    value = 0.5 * x * (1.0 + k)
    slope = 0.5 * (1.0 + k) + 0.5 * x * (1.0 - k * k) * GELU_SCALE * (1.0 + 3.0 * CUBIC_TERM * x * x)
    return value, slope


def iota(shape, dim):
    return lax.broadcasted_iota(jnp.int32, shape, dim)


def vm(*shape, dtype=BF):
    return pltpu.VMEM(shape, dtype)


def sems(*shape):
    return pltpu.SemaphoreType.DMA(shape)


SCRATCH = dict(
    hid=vm(ROWS, WIDTH), w_out=vm(WIDTH, WIDTH), f_in=vm(512, WIDTH), f_out=vm(512, WIDTH),
    qh=vm(8, ROWS, HEAD), kh=vm(SRC_ALL, HEAD), vh=vm(SRC_ALL, HEAD), att_in=vm(8, ROWS, HEAD),
    att_send=vm(8, ROWS, HEAD), vT=vm(HEAD + 16, SRC_ALL), kT=vm(HEAD, SRC_ALL), sbuf=vm(SRC_ALL, ROWS, dtype=F32),
    pall=vm(8, SRC_ALL, ROWS), dsbuf=vm(SRC_ALL, ROWS),
    oT=vm(8, HEAD, ROWS), stat=vm(8, 8, ROWS, dtype=F32), att=vm(ROWS, WIDTH),
    mixed=vm(ROWS, WIDTH, dtype=F32), xin=vm(ROWS, WIDTH), hitT=vm(ROWS, ROWS),
    xs=vm(ROWS, ROWS), gs=vm(ROWS, ROWS), ms=vm(HEAD, HEAD, dtype=F32),
    xr=vm(ROWS, ROWS), gr=vm(ROWS, ROWS), mr=vm(HEAD, HEAD, dtype=F32),
    xall=vm(2, 256, WIDTH), gall=vm(2, 256, WIDTH), mall=vm(8, 16, HEAD, dtype=F32),
    backT=vm(512, 512, dtype=F32), actg=vm(512, 512), dpT=vm(512, 512), dpr=vm(512, 512),
    part=vm(2, 256, WIDTH), pr=vm(8, 64, WIDTH), gps=vm(2, 2, 8, HEAD, dtype=F32), gpr=vm(8, 2, 8, HEAD, dtype=F32),
    ps=vm(ROWS, ROWS), br=vm(ROWS, ROWS), gsum=vm(2, 8, HEAD, dtype=F32), gb=vm(HEAD, HEAD, dtype=F32),
    dhid=vm(ROWS, WIDTH), d_fin=vm(512, WIDTH), d_fout=vm(512, WIDTH),
    og=vm(8, ROWS, HEAD), ogr=vm(8, ROWS, HEAD), dqs=vm(8, ROWS, HEAD), dqr=vm(8, ROWS, HEAD),
    dka=vm(SRC_ALL, HEAD, dtype=F32), dva=vm(SRC_ALL, HEAD, dtype=F32), dks=vm(SRC_ALL, HEAD), dvs=vm(SRC_ALL, HEAD),
    dkr=vm(8, HEAD, HEAD), dvr=vm(8, HEAD, HEAD),
    w1=vm(8, 2, 64, WIDTH), c1=vm(8, 64, WIDTH), x5=vm(3, 8, WIDTH, dtype=F32),
    wtmp=vm(8, 64, 512, dtype=F32), ya=vm(8, 64, 512), yar=vm(4, 2, 64, 512), sa=vm(8, 16, 512), sar=vm(8, 16, 512),
    sb=vm(8, 64, 512), sbr=vm(8, 64, 512), yb=vm(4, 16, 512), ybr=vm(4, 16, 512),
    r1=vm(16, 64, HEAD), r1r=vm(16, 64, HEAD), r2=vm(8, 64, HEAD), r3=vm(16, 64, HEAD),
    g1=vm(8, 8, HEAD, dtype=F32), g2=vm(16, 8, HEAD, dtype=F32),
    dw=vm(8, WIDTH, dtype=F32), d_router=vm(WIDTH, HEAD, dtype=F32), d_gain=vm(8, HEAD, dtype=F32),
    dout=vm(ROWS, WIDTH),
    k_sem=sems(2), v_sem=sems(2), qn_sem=sems(2), qf_sem=sems(2), a_sem=sems(2), x_sem=sems(2), g_sem=sems(2),
    m_sem=sems(2), xan_sem=sems(2), xaf_sem=sems(2), ga_sem=sems(2), ma_sem=sems(2), p_sem=sems(2),
    gp_sem=sems(2), p2_sem=sems(2), b_sem=sems(2), gb_sem=sems(2), ogn_sem=sems(2), ogf_sem=sems(2), dq_sem=sems(2),
    dk_sem=sems(2), dv_sem=sems(2), c_sem=sems(2), xh_sem=sems(2), ya_sem=sems(2), yb_sem=sems(2), sa_sem=sems(2),
    sb_sem=sems(2), r1_sem=sems(2), r2_sem=sems(2), r3_sem=sems(2), g1_sem=sems(2), g2_sem=sems(2),
    io_sem=sems(17),
)
INPUTS = (
    "length", "gain", "router", "ids", "slots", "q", "k", "v", "dout_hbm", "hid_hbm", "w_out_hbm",
    "f_in_hbm", "f_out_hbm",
)
OUTPUTS = (
    "dhid_hbm", "dq_hbm", "dk_hbm", "dv_hbm", "dw_hbm", "d_router_hbm", "d_gain_hbm", "d_fin_hbm",
    "d_fout_hbm",
)


class Refs:
    pass


def block_kernel(*refs):
    R = Refs()
    for name, ref in zip(INPUTS + OUTPUTS + tuple(SCRATCH), refs, strict=True):
        setattr(R, name, ref)
    src, tok = lax.axis_index("src"), lax.axis_index("tok")
    y_me, x_me, c_me = tok // 4, (tok // 2) % 2, tok % 2
    x_lo = src // 4

    loads = [
        pltpu.make_async_copy(a, b, R.io_sem.at[i])
        for i, (a, b) in enumerate(
            (
                (R.dout_hbm, R.dout), (R.hid_hbm, R.hid), (R.w_out_hbm, R.w_out), (R.f_out_hbm, R.f_out), (R.f_in_hbm, R.f_in),
                (R.k.at[:, lanes(src)], R.kh.at[rows(src, 128)]), (R.v.at[:, lanes(src)], R.vh.at[rows(src, 128)]),
                (R.q.at[:, lanes(src)], R.qh.at[src]),
            )
        )
    ]
    for copy in loads:
        copy.start()
    greet(src, tok)

    def by_src(*way):
        return Swap("src", src, *way)

    def by_tok(*way):
        return Swap("tok", tok, *way)

    def first(ref, size=1):
        return lambda n: ref.at[pl.ds(0, n * size)]

    def at(ref):
        return lambda i: ref.at[i]

    def at_rows(ref, size):
        return lambda i: ref.at[rows(i, size)]

    k_swap = by_src(R.k_sem, lambda p: R.k.at[:, lanes(p)], at_rows(R.kh, 128), first(R.kh, 128))
    v_swap = by_src(R.v_sem, lambda p: R.v.at[:, lanes(p)], at_rows(R.vh, 128), first(R.vh, 128))
    q_way = lambda p: R.q.at[:, lanes(p)], at(R.qh), first(R.qh)
    q_near, q_far = by_src(R.qn_sem, *q_way, 1, 4, near_step), by_src(R.qf_sem, *q_way, 4, 8, far_step)
    a_swap = by_src(R.a_sem, at(R.att_send), at(R.att_in), first(R.att_in))
    x_swap = by_tok(R.x_sem, at_rows(R.xs, 16), at_rows(R.xr, 16), first(R.xr, 16))
    g_swap = by_tok(R.g_sem, at_rows(R.gs, 16), at_rows(R.gr, 16), first(R.gr, 16))
    m_swap = by_tok(R.m_sem, at_rows(R.ms, 8), at_rows(R.mr, 8), first(R.mr, 8))
    def xa_half(sem, half):
        return by_src(
            sem, lambda p: R.xall.at[half, rows(src, 32)], lambda i: R.xall.at[half, rows(i, 32)],
            lambda n: R.xall.at[half, pl.ds(0, n * 32)],
        )

    def p_half(sem, half):
        return by_src(
            sem, lambda p: R.part.at[half, rows(p, 32)], lambda i: R.pr.at[i, pl.ds(half * 32, 32)],
            lambda n: R.pr.at[pl.ds(0, n), pl.ds(half * 32, 32)],
        )

    xa_swaps = xa_half(R.xan_sem, 0), xa_half(R.xaf_sem, 1)
    p_swaps = p_half(R.p_sem, 0), p_half(R.p2_sem, 1)
    ga_swap = by_src(
        R.ga_sem, lambda p: R.gall.at[:, rows(src, 32)], lambda i: R.gall.at[:, rows(i, 32)],
        lambda n: R.gall.at[:, pl.ds(0, n * 32)],
    )
    ma_swap = by_src(R.ma_sem, lambda p: R.mall.at[src], at(R.mall), first(R.mall))
    gp_swap = by_src(R.gp_sem, lambda p: R.gps.at[p // 4], at(R.gpr), first(R.gpr))
    b_swap = by_tok(R.b_sem, at_rows(R.ps, 16), at_rows(R.br, 16), first(R.br, 16))
    gb_swap = by_tok(R.gb_sem, lambda p: R.gsum.at[p // 8], at_rows(R.gb, 8), first(R.gb, 8))
    og_way = at(R.og), at(R.ogr), first(R.ogr)
    og_near, og_far = by_src(R.ogn_sem, *og_way, 1, 4, near_step), by_src(R.ogf_sem, *og_way, 4, 8, far_step)
    dq_swap = by_src(R.dq_sem, at(R.dqs), at(R.dqr), first(R.dqr))
    dk_swap = by_src(R.dk_sem, at_rows(R.dks, 128), at(R.dkr), first(R.dkr))
    dv_swap = by_src(R.dv_sem, at_rows(R.dvs, 128), at(R.dvr), first(R.dvr))
    sa_swap = by_src(R.sa_sem, at(R.sa), at(R.sar), first(R.sar))
    sb_swap = by_src(R.sb_sem, at(R.sb), at(R.sbr), first(R.sbr))
    r1_swap = by_tok(R.r1_sem, at(R.r1), at(R.r1r), first(R.r1r))
    r2_swap = by_src(R.r2_sem, lambda p: R.r2.at[src], at(R.r2), first(R.r2))
    r3_swap = by_tok(R.r3_sem, lambda p: R.r3.at[tok], at(R.r3), first(R.r3))
    g1_swap = by_src(R.g1_sem, lambda p: R.g1.at[src], at(R.g1), first(R.g1))
    g2_swap = by_tok(R.g2_sem, lambda p: R.g2.at[tok], at(R.g2), first(R.g2))

    def y_go(sem, source, target, held):
        def send(k):
            to = tok_step(tok, 4 * k)
            remote(source(to // 4), target(y_me), sem.at[0], sem.at[1], "tok", to).start()

        each(4, send)

    def y_arrive(sem, source, target, held):
        bulk_wait(held, sem.at[1])

    def y_sent(sem, source, target, held):
        bulk_wait(held, sem.at[0])

    ya_way = (R.ya_sem, lambda y: R.ya.at[pl.ds(y * 2, 2)], at(R.yar), R.yar.at[pl.ds(0, 3)])
    yb_way = (R.yb_sem, at(R.yb), at(R.ybr), R.ybr.at[pl.ds(0, 3)])

    k_swap.send_all()
    v_swap.send_all()

    def aim_of(id_of, slot_of):
        return jnp.where((id_of < N_TOK) & (slot_of >= 0), id_of * CAP + slot_of, -1)

    j = iota((ROWS, ROWS), 0)
    key = (j // 16) * CAP + j % CAP
    aim_rows = aim_of(R.ids[...], R.slots[...])
    hitT = jnp.where((aim_rows[0:1, :] == key) | (aim_rows[1:2, :] == key), 1.0, 0.0)
    R.hitT[...] = hitT.astype(BF)
    row_blk = (j // CAP) % 4
    zero = jnp.zeros((ROWS, ROWS), BF)

    def to_experts(ref, out):
        acc = None
        for b in range(4):
            term = nn(jnp.where(row_blk == b, R.hitT[...], zero), ref[:, b * 256 : (b + 1) * 256])
            acc = term if acc is None else acc + term
        out[...] = acc.astype(BF)

    loads[0].wait()
    to_experts(R.dout, R.gs)
    g_swap.send_all()
    k_swap.sent_all()
    v_swap.sent_all()
    q_near.send_all()
    q_near.sent_all()
    q_far.send_all()
    R.gr[rows(tok, 16), :] = R.gs[rows(tok, 16), :]
    for copy in loads[5:]:
        copy.wait()
    k_swap.arrive_all()
    v_swap.arrive_all()
    length = R.length[tok]
    seen = iota((SRC_ALL, HEAD), 0) < length
    seen_row = iota((HEAD, SRC_ALL), 1) < length
    k_wide = R.kh[...].astype(F32)
    R.kh[...] = jnp.where(seen, k_wide, k_wide[0:1, :]).astype(BF)
    R.vT[:HEAD, :] = jnp.where(seen_row, R.vh[...].astype(F32).T, 0.0).astype(BF)
    R.vT[HEAD:, :] = jnp.where(seen_row[:16], 1.0, 0.0).astype(BF)

    def forward_block(b):
        q = R.qh[b]
        top = jnp.full((8, ROWS), -3e38, F32)
        for c in range(0, SRC_ALL, 128):
            s = nt(R.kh[c : c + 128, :], q)
            R.sbuf[c : c + 128, :] = s
            top = jnp.maximum(top, fold8(s, jnp.max))
        top = jnp.max(top, axis=0, keepdims=True)
        for c in range(0, SRC_ALL, 128):
            p = jnp.exp2((R.sbuf[c : c + 128, :] - top) * EXP2_SCALE)
            R.pall[b, c : c + 128, :] = p.astype(BF)
        summed = nn(R.vT[...], R.pall[b])
        inv = 1.0 / summed[HEAD : HEAD + 1, :]
        oT = summed[:HEAD, :] * inv
        R.oT[b] = oT.astype(BF)
        R.stat[b] = jnp.broadcast_to(inv, (8, ROWS))
        R.att_send[b] = oT.T.astype(BF)

    i64, j256 = iota((64, ROWS), 0), iota((64, ROWS), 1)
    take = [jnp.where(j256 == (i64 // CAP) * 16 + b * CAP + i64 % CAP, 1.0, 0.0).astype(BF) for b in range(4)]

    def unpack(got, out):
        for b in range(4):
            block = nn(take[b], got[...]).astype(BF)
            out[0, rows(src, 32), b * 256 : (b + 1) * 256] = block[:32]
            out[1, rows(src, 32), b * 256 : (b + 1) * 256] = block[32:]

    def g_on():
        g_swap.arrive_all()
        unpack(R.gr, R.gall)
        ga_swap.send_all()

    forward_block(src)
    R.att_in[src] = R.att_send[src]

    def forward_turn(k):
        forward_block(src_step(src, k, True))
        a_swap.send(src_step(0, k, True))

    q_near.arrive_all()
    each(4, lambda i: forward_turn(near_step(i)))
    q_far.arrive_all()
    each(8, lambda i: forward_turn(far_step(i)), 4)

    id_cols = jnp.concatenate([R.ids[...], R.slots[...], R.ids[...], R.slots[...]], axis=0).astype(F32).T
    id_cols = id_cols.astype(jnp.int32)
    id1, id2, slot1, slot2 = (id_cols[:, i : i + 1] for i in range(4))
    lane = iota((ROWS, HEAD), 1)
    pick1 = jnp.where(id1 == lane, 1.0, 0.0)
    pick2 = jnp.where(id2 == lane, 1.0, 0.0)
    live1, live2 = slot1 >= 0, slot2 >= 0
    base = (src % 4) * 32 + (tok % 8) * CAP
    own1 = jnp.where(live1 & (id1 < N_TOK) & (id1 == lane // 8), 1.0, 0.0)
    own2 = jnp.where(live2 & (id2 < N_TOK) & (id2 == lane // 8), 1.0, 0.0)
    at1 = jnp.where(live1 & (lane == base + slot1), 1.0, 0.0)
    at2 = jnp.where(live2 & (lane == base + slot2), 1.0, 0.0)
    for copy in loads[1:5]:
        copy.wait()
    a_swap.arrive_all()
    for h in range(N_SRC):
        R.att[:, h * HEAD : (h + 1) * HEAD] = R.att_in[h]

    R.mixed[...] = R.hid[...].astype(F32) + nn(R.att[...], R.w_out[...])
    inv_parts = []
    for r in range(0, ROWS, 64):
        m = R.mixed[r : r + 64, :]
        centred = m - jnp.mean(m, axis=1, keepdims=True)
        inv = lax.rsqrt(jnp.mean(centred * centred, axis=1, keepdims=True) + NORM_EPS)
        inv_parts.append(inv)
        normed = centred * inv
        R.mixed[r : r + 64, :] = normed
        R.xin[r : r + 64, :] = (normed * R.gain[...]).astype(BF)
    inv_std = jnp.concatenate(inv_parts, axis=0)
    to_experts(R.xin, R.xs)
    x_swap.send_all()
    g_on()
    R.xr[rows(tok, 16), :] = R.xs[rows(tok, 16), :]
    logits = nn(R.xin[...], R.router[...])
    gap = jnp.sum(logits * (pick1 - pick2), axis=1, keepdims=True)
    gate1 = 1.0 / (1.0 + jnp.exp(-gap))
    gate2 = 1.0 / (1.0 + jnp.exp(gap))
    low1 = gate1.astype(BF).astype(F32)
    low2 = gate2.astype(BF).astype(F32)
    R.ms[...] = nn((own1 * low1).T.astype(BF), at1.astype(BF)) + nn((own2 * low2).T.astype(BF), at2.astype(BF))
    m_swap.send_all()
    R.mr[rows(tok, 8), :] = R.ms[rows(tok, 8), :]
    for swap in (q_far, a_swap, g_swap):
        swap.sent_all()

    x_swap.arrive_all()
    unpack(R.xr, R.xall)
    xa_swaps[0].send_all()
    m_swap.arrive_all()
    R.mall[src] = jnp.concatenate([fold8(R.mr[:64, :], jnp.sum), fold8(R.mr[64:, :], jnp.sum)], axis=0)
    ma_swap.send_all()
    ga_swap.arrive_all()
    for c in range(0, 512, 128):
        R.backT[c : c + 128, :] = nt(R.f_out[c : c + 128, :], R.gall[...].reshape(512, WIDTH))
    R.kT[...] = jnp.where(seen_row, R.kh[...].astype(F32).T, 0.0).astype(BF)
    xa_swaps[0].sent_all()
    xa_swaps[1].send_all()
    for swap in (x_swap, m_swap, ga_swap):
        swap.sent_all()
    ma_swap.arrive_all()

    for half in range(2):
        xa_swaps[half].arrive_all()
        here = slice(half * 256, (half + 1) * 256)
        x_half = R.xall[half]
        gates = jnp.sum(R.mall[:, half * 8 : half * 8 + 8, :].reshape(2, 4, 8, HEAD), axis=1)
        gate_row = jnp.concatenate([gates[0, 0:1, :], gates[1, 0:1, :]], axis=1)
        gate_acc = jnp.zeros((8, 256), F32)
        for c in range(0, 512, 128):
            value, slope = gelu_pair(nt(R.f_in[c : c + 128, :], x_half))
            act = value.astype(BF).astype(F32)
            back = R.backT[c : c + 128, here]
            gate_acc = gate_acc + fold8(back * act, jnp.sum)
            R.actg[c : c + 128, here] = (act * gate_row).astype(BF)
            dp = gate_row * back * slope
            R.dpT[c : c + 128, here] = dp.astype(BF)
            R.dpr[here, c : c + 128] = dp.T.astype(BF)
        gate_tot = jnp.sum(gate_acc, axis=0, keepdims=True)
        R.gps[0, half] = jnp.broadcast_to(gate_tot[:, :HEAD], (8, HEAD))
        R.gps[1, half] = jnp.broadcast_to(gate_tot[:, HEAD:], (8, HEAD))
        R.part[half] = nn(R.dpr[here, :], R.f_in[...]).astype(BF)
        p_swaps[half].send_all()
        R.pr[src, half * 32 : half * 32 + 32, :] = R.part[half, rows(src, 32), :]
    gp_swap.send_all()
    R.gpr[src] = R.gps[src // 4]
    stores = [
        pltpu.make_async_copy(a, b, R.io_sem.at[8 + i])
        for i, (a, b) in enumerate(
            (
                (R.d_fin, R.d_fin_hbm), (R.d_fout, R.d_fout_hbm), (R.dhid, R.dhid_hbm),
                (R.dw, R.dw_hbm), (R.d_router, R.d_router_hbm), (R.d_gain, R.d_gain_hbm),
            )
        )
    ]
    for c in range(0, 512, 128):
        R.d_fin[c : c + 128, :] = nn(R.dpT[c : c + 128, :], R.xall[...].reshape(512, WIDTH)).astype(BF)
        R.d_fout[c : c + 128, :] = nn(R.actg[c : c + 128, :], R.gall[...].reshape(512, WIDTH)).astype(BF)
    stores[0].start()
    stores[1].start()
    for swap in (xa_swaps[1], ma_swap):
        swap.sent_all()
    gp_swap.arrive_all()
    R.gsum[...] = jnp.sum(R.gpr[...], axis=0)
    gb_swap.send_all()
    R.gb[rows(tok, 8), :] = R.gsum[tok // 8]
    p_swaps[0].arrive_all()
    p_swaps[1].arrive_all()
    acc = None
    for b in range(4):
        blk = jnp.sum(R.pr[:, :, b * 256 : (b + 1) * 256].astype(F32), axis=0).astype(BF)
        term = nn(take[b].astype(F32).T.astype(BF), blk)
        acc = term if acc is None else acc + term
    R.ps[...] = acc.astype(BF)
    b_swap.send_all()
    R.br[rows(tok, 16), :] = R.ps[rows(tok, 16), :]

    gb_swap.arrive_all()
    first = jnp.where(lane % 8 == 0, 1.0, 0.0)
    got1 = nn(own1 * first, R.gb[...], precision=lax.Precision.HIGHEST)
    got2 = nn(own2 * first, R.gb[...], precision=lax.Precision.HIGHEST)
    grad1 = jnp.sum(got1 * at1, axis=1, keepdims=True)
    grad2 = jnp.sum(got2 * at2, axis=1, keepdims=True)
    logit_grad = gate1 * gate2 * (grad1 - grad2)
    column = (pick1 - pick2) * logit_grad
    col_hi = column.astype(BF)
    col_lo = (column - col_hi.astype(F32)).astype(BF)
    colT = column.T
    colT_hi = colT.astype(BF)
    colT_lo = (colT - colT_hi.astype(F32)).astype(BF)
    router_part = (nn(colT_hi, R.xin[...]) + nn(colT_lo, R.xin[...])).T.astype(BF)
    for t in range(N_TOK):
        R.r1[t] = router_part[t * 64 : (t + 1) * 64, :]
    r1_swap.send_all()
    R.r1r[tok] = R.r1[tok]
    for swap in (*p_swaps, gp_swap, gb_swap):
        swap.sent_all()
    b_swap.arrive_all()

    scaled_sum = jnp.zeros((ROWS, 1), F32)
    cross_sum = jnp.zeros((ROWS, 1), F32)
    scaled_all = []
    gain_rows = []
    for b in range(4):
        cut = slice(b * 256, (b + 1) * 256)
        mine = jnp.where(row_blk == b, R.hitT[...], zero)
        total = lax.dot_general(mine, R.br[...], (((0,), (0,)), ((), ())), preferred_element_type=F32)
        total = total + nt(col_hi, R.router[cut, :]) + nt(col_lo, R.router[cut, :])
        normed = R.mixed[:, cut]
        row = jnp.sum(total * normed, axis=0, keepdims=True)
        gain_rows += [row[:, :HEAD], row[:, HEAD:]]
        scaled = total * R.gain[:, cut]
        scaled_all.append(scaled)
        scaled_sum = scaled_sum + jnp.sum(scaled, axis=1, keepdims=True)
        cross_sum = cross_sum + jnp.sum(scaled * normed, axis=1, keepdims=True)
    mean1 = scaled_sum * (1.0 / WIDTH)
    mean2 = cross_sum * (1.0 / WIDTH)
    for b in range(4):
        cut = slice(b * 256, (b + 1) * 256)
        R.dhid[:, cut] = (
            R.dout[:, cut].astype(F32) + inv_std * (scaled_all[b] - mean1 - R.mixed[:, cut] * mean2)
        ).astype(BF)
    for h in range(N_SRC):
        R.og[h] = nt(R.dhid[...], R.w_out[h * HEAD : (h + 1) * HEAD, :]).astype(BF)
    og_near.send_all()
    og_far.send_all()
    R.g1[src] = jnp.concatenate(gain_rows, axis=0)
    g1_swap.send_all()
    stores[2].start()
    R.ogr[src] = R.og[src]

    for i in range(8):
        cut = slice(i * HEAD, (i + 1) * HEAD)
        w = nn(R.att[:, cut].astype(F32).T.astype(BF), R.dhid[...]).astype(BF)
        R.w1[i, 0] = w[:64]
        R.w1[i, 1] = w[64:]
    core_copy = remote(R.w1.at[:, 1 - c_me], R.c1, R.c_sem.at[0], R.c_sem.at[1], "tok", tok_step(tok, 1))
    core_copy.start()
    R.dka[...] = jnp.zeros_like(R.dka)
    R.dva[...] = jnp.zeros_like(R.dva)

    def backward_block(b):
        q, d_o = R.qh[b], R.ogr[b]
        d_wide = d_o.astype(F32)
        row_term = jnp.sum(d_wide.T * R.oT[b].astype(F32), axis=0, keepdims=True)
        factor = R.stat[b][0:1, :] * FACTOR
        scaled_d = (d_wide * R.stat[b].T[:, 0:1]).astype(BF)
        for c in range(0, SRC_ALL, 128):
            p = R.pall[b, c : c + 128, :].astype(F32)
            dp = nt(R.vh[c : c + 128, :], d_o)
            R.dsbuf[c : c + 128, :] = (p * ((dp - row_term) * factor)).astype(BF)
        R.dqs[b] = nn(R.kT[...], R.dsbuf[...]).T.astype(BF)
        R.dka[...] += nn(R.dsbuf[...], q)
        R.dva[...] += nn(R.pall[b], scaled_d)

    def backward_turn(k):
        backward_block(src_step(src, k, True))
        dq_swap.send(src_step(0, k, True))

    def turns(low, high):
        pick = near_step if high <= 4 else far_step
        each(high, lambda i: backward_turn(pick(i)), low)

    backward_block(src)
    R.dqr[src] = R.dqs[src]
    core_copy.wait_recv()
    for i in range(8):
        piece = R.w1[i, c_me].astype(F32) + R.c1[i].astype(F32)
        R.ya[i] = piece[:, :512].astype(BF)
        R.wtmp[i] = piece[:, 512:]
    y_go(*ya_way)
    for s in range(N_SRC):
        R.sb[s] = jnp.concatenate([R.wtmp[i, s * 8 : (s + 1) * 8, :] for i in range(8)], axis=0).astype(BF)
    sb_swap.send_all()
    R.yar[y_me] = R.ya[pl.ds(y_me * 2, 2)]
    R.sbr[src] = R.sb[src]
    r1_swap.arrive_all()
    R.r2[src] = jnp.sum(R.r1r[...].astype(F32), axis=0).astype(BF)
    r2_swap.send_all()
    og_near.arrive_all()
    turns(1, 4)
    g1_swap.arrive_all()
    R.g2[tok] = jnp.sum(R.g1[...], axis=0)
    g2_swap.send_all()
    r2_swap.arrive_all()
    R.r3[tok] = jnp.sum(R.r2[...].astype(F32), axis=0).astype(BF)
    r3_swap.send_all()
    og_far.arrive_all()
    turns(4, 6)
    y_arrive(*ya_way)
    a0 = jnp.sum(R.yar[:, 0].astype(F32), axis=0)
    a1 = jnp.sum(R.yar[:, 1].astype(F32), axis=0)
    for s in range(N_SRC):
        R.sa[s] = jnp.concatenate([a0[s * 8 : (s + 1) * 8, :], a1[s * 8 : (s + 1) * 8, :]], axis=0).astype(BF)
    sa_swap.send_all()
    R.sar[src] = R.sa[src]
    sb_swap.arrive_all()
    sums = jnp.sum(R.sbr[...].astype(F32), axis=0)
    for y in range(4):
        R.yb[y] = sums[y * 16 : (y + 1) * 16, :].astype(BF)
    y_go(*yb_way)
    R.ybr[y_me] = R.yb[y_me]
    turns(6, 8)
    R.dks[...] = jnp.where(seen, R.dka[...], 0.0).astype(BF)
    dk_swap.send_all()
    R.dvs[...] = jnp.where(seen, R.dva[...], 0.0).astype(BF)
    dv_swap.send_all()
    R.dkr[src] = R.dks[rows(src, 128), :]
    R.dvr[src] = R.dvs[rows(src, 128), :]
    sa_swap.arrive_all()
    y_arrive(*yb_way)
    sums_a = jnp.sum(R.sar[...].astype(F32), axis=0)
    sums_b = jnp.sum(R.ybr[...].astype(F32), axis=0)
    for x in range(2):
        R.x5[x, :, :512] = sums_a[x * 8 : (x + 1) * 8, :]
        R.x5[x, :, 512:] = sums_b[x * 8 : (x + 1) * 8, :]
    x_copy = remote(R.x5.at[1 - x_me], R.x5.at[2], R.xh_sem.at[0], R.xh_sem.at[1], "tok", tok_step(tok, 2))
    x_copy.start()
    for swap in (b_swap, r1_swap, og_near, og_far, r2_swap, g1_swap, sb_swap, sa_swap):
        swap.sent_all()
    core_copy.wait_send()
    y_sent(*ya_way)
    y_sent(*yb_way)

    def keep(swap, held, out, sem):
        swap.arrive_all()
        for h in range(N_SRC):
            pltpu.make_async_copy(held.at[h], out.at[:, pl.ds(h * HEAD, HEAD)], sem).start()

    keep(dq_swap, R.dqr, R.dq_hbm, R.io_sem.at[14])
    g2_swap.arrive_all()
    R.d_gain[...] = jnp.sum(R.g2[...], axis=0)
    r3_swap.arrive_all()
    for t in range(N_TOK):
        R.d_router[t * 64 : (t + 1) * 64, :] = R.r3[t].astype(F32)
    stores[4].start()
    stores[5].start()
    x_copy.wait_recv()
    R.dw[...] = R.x5[x_me] + R.x5[2]
    stores[3].start()
    keep(dk_swap, R.dkr, R.dk_hbm, R.io_sem.at[15])
    keep(dv_swap, R.dvr, R.dv_hbm, R.io_sem.at[16])
    for swap in (r3_swap, g2_swap, dq_swap, dk_swap, dv_swap):
        swap.sent_all()
    x_copy.wait_send()
    bulk_wait(R.dqr, R.io_sem.at[14])
    bulk_wait(R.dkr, R.io_sem.at[15])
    bulk_wait(R.dvr, R.io_sem.at[16])
    for copy in stores:
        copy.wait()


def hand_over_kernel(*refs):
    count = (len(refs) - 1) // 3
    given, out, held, sem = refs[:count], refs[count : 2 * count], refs[2 * count : 3 * count], refs[-1]
    order = sorted(range(count), key=lambda i: -given[i].size)
    loads = [pltpu.make_async_copy(given[i], held[i], sem.at[0, i]) for i in order]
    stores = [pltpu.make_async_copy(held[i], out[i], sem.at[1, i]) for i in order]
    for copy in loads:
        copy.start()
    for load, store in zip(loads, stores):
        load.wait()
        store.start()
    for copy in stores:
        copy.wait()


VMEM = pl.BlockSpec(memory_space=pltpu.VMEM)
SMEM = pl.BlockSpec(memory_space=pltpu.SMEM)
HBM = pl.BlockSpec(memory_space=pl.ANY)


def on_device(
    hidden_in, d_out, queries, keys, values, source_len, out_weight, norm_gain, router,
    expert_ids, expert_slots, fc_in, fc_out,
):
    shapes = tuple(
        jax.ShapeDtypeStruct(s, d)
        for s, d in (
            ((ROWS, WIDTH), BF), ((ROWS, WIDTH), BF), ((HEAD, WIDTH), BF), ((HEAD, WIDTH), BF), ((8, WIDTH), F32),
            ((WIDTH, HEAD), F32), ((8, HEAD), F32), ((512, WIDTH), BF), ((512, WIDTH), BF),
        )
    )
    outs = pl.pallas_call(
        block_kernel,
        out_shape=shapes,
        in_specs=[SMEM] + [VMEM] * 4 + [HBM] * 8,
        out_specs=(HBM,) * 9,
        scratch_shapes=list(SCRATCH.values()),
        compiler_params=pltpu.CompilerParams(
            collective_id=1, has_side_effects=True, vmem_limit_bytes=58 * 1024 * 1024
        ),
    )(
        source_len, norm_gain[None], router, expert_ids.T, expert_slots.T, queries, keys[0], values[0], d_out,
        hidden_in, out_weight, fc_in[0], fc_out[0],
    )
    dhid, dq, dk, dv, dw, d_router, d_gain, d_fin, d_fout = pl.pallas_call(
        hand_over_kernel,
        out_shape=shapes,
        in_specs=[HBM] * 9,
        out_specs=(HBM,) * 9,
        scratch_shapes=[pltpu.VMEM(s.shape, s.dtype) for s in shapes] + [sems(2, 9)],
        compiler_params=pltpu.CompilerParams(vmem_limit_bytes=58 * 1024 * 1024),
    )(*outs)
    return dhid, dq, dk[None], dv[None], dw, d_router, d_gain.reshape(-1), d_fin[None], d_fout[None]


def solution(mesh):
    return jax.shard_map(
        on_device,
        mesh=mesh,
        in_specs=(
            P(("tok", "src"), None), P(("tok", "src"), None), P(("tok", "src"), None),
            P("tok", "src", None), P("tok", "src", None), P(), P(), P(), P(),
            P(("tok", "src"), None), P(("tok", "src"), None), P("tok", "src", None), P("tok", "src", None),
        ),
        out_specs=(
            P(("tok", "src"), None), P(("tok", "src"), None), P("tok", "src", None), P("tok", "src", None),
            P(("tok", "src"), None), P(), P(), P("tok", "src", None), P("tok", "src", None),
        ),
        check_vma=False,
    )
```

```python
import math

import jax
import jax.numpy as jnp
from jax import lax
from jax.experimental import pallas as pl
from jax.experimental.pallas import tpu as pltpu
from jax.sharding import PartitionSpec as P

MESH = pl.DeviceIdType.MESH
BF, F32 = jnp.bfloat16, jnp.float32
HEAD = 128
CAP = 4
NORM_EPS = 1e-05
GELU_SCALE = 0.7978845608028654
CUBIC_TERM = 0.044715
FACTOR = 1.0 / math.sqrt(HEAD)
EXP2_SCALE = FACTOR / math.log(2.0)
MASKED = -1e30
N_SRC, N_TOK = 8, 16
ROWS, WIDTH, SRC_ALL = 256, 1024, 1024


def nn(a, b, **kw):
    return lax.dot_general(a, b, (((1,), (0,)), ((), ())), preferred_element_type=F32, **kw)


def nt(a, b, **kw):
    return lax.dot_general(a, b, (((1,), (1,)), ((), ())), preferred_element_type=F32, **kw)


def src_step(src, k, back=False):
    x, z = src // 4, src % 4
    z = (z + 4 - k % 4) % 4 if back else (z + k % 4) % 4
    return ((x + k // 4) % 2) * 4 + z


def tok_step(tok, k, back=False):
    y, x, c = tok // 4, (tok // 2) % 2, tok % 2
    y = (y + 4 - k // 4) % 4 if back else (y + k // 4) % 4
    return y * 4 + ((x + (k // 2) % 2) % 2) * 2 + (c + k % 2) % 2


def remote(src_ref, dst_ref, send_sem, recv_sem, axis, peer):
    return pltpu.make_async_remote_copy(
        src_ref=src_ref,
        dst_ref=dst_ref,
        send_sem=send_sem,
        recv_sem=recv_sem,
        device_id={axis: peer},
        device_id_type=MESH,
    )


def each(count, body, low=1):
    def step(k, carry):
        body(k)
        return carry

    lax.fori_loop(low, count, step, 0)


def greet(src, tok):
    bar = pltpu.get_barrier_semaphore()
    waits = 0
    if src is not None:
        waits += N_SRC - 1
        each(N_SRC, lambda k: pl.semaphore_signal(bar, inc=1, device_id={"src": src_step(src, k)}, device_id_type=MESH))
    if tok is not None:
        waits += N_TOK - 1
        each(N_TOK, lambda k: pl.semaphore_signal(bar, inc=1, device_id={"tok": tok_step(tok, k)}, device_id_type=MESH))
    pl.semaphore_wait(bar, waits)


class Swap:
    def __init__(self, axis, me, sems, source, target, blocks, low=1, high=None, pick=None):
        self.pick = pick or (lambda i: i)
        self.axis, self.me, self.sems = axis, me, sems
        self.source, self.target = source, target
        self.low, self.high = low, high or (N_SRC if axis == "src" else N_TOK)
        self.held = blocks(self.high - low)
        self.step = src_step if axis == "src" else tok_step

    def send(self, k):
        to = self.step(self.me, self.pick(k))
        remote(self.source(to), self.target(self.me), self.sems.at[0], self.sems.at[1], self.axis, to).start()

    def send_all(self):
        each(self.high, self.send, self.low)

    def arrive_all(self):
        bulk_wait(self.held, self.sems.at[1])

    def sent_all(self):
        bulk_wait(self.held, self.sems.at[0])


def near_step(i):
    return 2 * i - 1 - (i - 1) // 2


def far_step(i):
    return i - 2 + 2 * ((i - 2) // 3)


def bulk_wait(ref, sem):
    pltpu.make_async_copy(ref, ref, sem).wait()


def lanes(index):
    return pl.ds(pl.multiple_of(index * HEAD, HEAD), HEAD)


def rows(index, size):
    return pl.ds(pl.multiple_of(index * size, size), size)


def fold8(value, op):
    return op(value.reshape(value.shape[0] // 8, 8, value.shape[1]), axis=0)


def gelu_pair(x):
    k = jnp.tanh(GELU_SCALE * (x + CUBIC_TERM * x * x * x))
    value = 0.5 * x * (1.0 + k)
    slope = 0.5 * (1.0 + k) + 0.5 * x * (1.0 - k * k) * GELU_SCALE * (1.0 + 3.0 * CUBIC_TERM * x * x)
    return value, slope


def iota(shape, dim):
    return lax.broadcasted_iota(jnp.int32, shape, dim)


def vm(*shape, dtype=BF):
    return pltpu.VMEM(shape, dtype)


def sems(*shape):
    return pltpu.SemaphoreType.DMA(shape)


SCRATCH = dict(
    hid=vm(ROWS, WIDTH), w_out=vm(WIDTH, WIDTH), f_in=vm(512, WIDTH), f_out=vm(512, WIDTH),
    qh=vm(8, ROWS, HEAD), kh=vm(SRC_ALL, HEAD), vh=vm(SRC_ALL, HEAD), att_in=vm(8, ROWS, HEAD),
    att_send=vm(8, ROWS, HEAD), vT=vm(HEAD + 16, SRC_ALL), kT=vm(HEAD, SRC_ALL), sbuf=vm(SRC_ALL, ROWS, dtype=F32),
    pall=vm(8, SRC_ALL, ROWS), dsbuf=vm(SRC_ALL, ROWS),
    oT=vm(8, HEAD, ROWS), stat=vm(8, 8, ROWS, dtype=F32), att=vm(ROWS, WIDTH),
    mixed=vm(ROWS, WIDTH, dtype=F32), xin=vm(ROWS, WIDTH), hitT=vm(ROWS, ROWS),
    xs=vm(ROWS, ROWS), gs=vm(ROWS, ROWS), ms=vm(HEAD, HEAD, dtype=F32),
    xr=vm(ROWS, ROWS), gr=vm(ROWS, ROWS), mr=vm(HEAD, HEAD, dtype=F32),
    xall=vm(2, 256, WIDTH), gall=vm(2, 256, WIDTH), mall=vm(8, 16, HEAD, dtype=F32),
    backT=vm(512, 512, dtype=F32), actg=vm(512, 512), dpT=vm(512, 512), dpr=vm(512, 512),
    part=vm(2, 256, WIDTH), pr=vm(8, 64, WIDTH), gps=vm(2, 2, 8, HEAD, dtype=F32), gpr=vm(8, 2, 8, HEAD, dtype=F32),
    ps=vm(ROWS, ROWS), br=vm(ROWS, ROWS), gsum=vm(2, 8, HEAD, dtype=F32), gb=vm(HEAD, HEAD, dtype=F32),
    dhid=vm(ROWS, WIDTH), d_fin=vm(512, WIDTH), d_fout=vm(512, WIDTH),
    og=vm(8, ROWS, HEAD), ogr=vm(8, ROWS, HEAD), dqs=vm(8, ROWS, HEAD), dqr=vm(8, ROWS, HEAD),
    dka=vm(SRC_ALL, HEAD, dtype=F32), dva=vm(SRC_ALL, HEAD, dtype=F32), dks=vm(SRC_ALL, HEAD), dvs=vm(SRC_ALL, HEAD),
    dkr=vm(8, HEAD, HEAD), dvr=vm(8, HEAD, HEAD),
    w1=vm(8, 2, 64, WIDTH), c1=vm(8, 64, WIDTH), x5=vm(3, 8, WIDTH, dtype=F32),
    wtmp=vm(8, 64, 512, dtype=F32), ya=vm(8, 64, 512), yar=vm(4, 2, 64, 512), sa=vm(8, 16, 512), sar=vm(8, 16, 512),
    sb=vm(8, 64, 512), sbr=vm(8, 64, 512), yb=vm(4, 16, 512), ybr=vm(4, 16, 512),
    r1=vm(16, 64, HEAD), r1r=vm(16, 64, HEAD), r2=vm(8, 64, HEAD), r3=vm(16, 64, HEAD),
    g1=vm(8, 8, HEAD, dtype=F32), g2=vm(16, 8, HEAD, dtype=F32),
    dw=vm(8, WIDTH, dtype=F32), d_router=vm(WIDTH, HEAD, dtype=F32), d_gain=vm(8, HEAD, dtype=F32),
    dout=vm(ROWS, WIDTH),
    k_sem=sems(2), v_sem=sems(2), qn_sem=sems(2), qf_sem=sems(2), a_sem=sems(2), x_sem=sems(2), g_sem=sems(2),
    m_sem=sems(2), xan_sem=sems(2), xaf_sem=sems(2), ga_sem=sems(2), ma_sem=sems(2), p_sem=sems(2),
    gp_sem=sems(2), p2_sem=sems(2), b_sem=sems(2), gb_sem=sems(2), ogn_sem=sems(2), ogf_sem=sems(2), dq_sem=sems(2),
    dk_sem=sems(2), dv_sem=sems(2), c_sem=sems(2), xh_sem=sems(2), ya_sem=sems(2), yb_sem=sems(2), sa_sem=sems(2),
    sb_sem=sems(2), r1_sem=sems(2), r2_sem=sems(2), r3_sem=sems(2), g1_sem=sems(2), g2_sem=sems(2),
    io_sem=sems(17),
)
INPUTS = (
    "length", "gain", "router", "ids", "slots", "q", "k", "v", "dout_hbm", "hid_hbm", "w_out_hbm",
    "f_in_hbm", "f_out_hbm",
)
OUTPUTS = (
    "dhid_hbm", "dq_hbm", "dk_hbm", "dv_hbm", "dw_hbm", "d_router_hbm", "d_gain_hbm", "d_fin_hbm",
    "d_fout_hbm",
)


class Refs:
    pass


def block_kernel(*refs):
    R = Refs()
    for name, ref in zip(INPUTS + OUTPUTS + tuple(SCRATCH), refs, strict=True):
        setattr(R, name, ref)
    src, tok = lax.axis_index("src"), lax.axis_index("tok")
    y_me, x_me, c_me = tok // 4, (tok // 2) % 2, tok % 2
    x_lo = src // 4

    loads = [
        pltpu.make_async_copy(a, b, R.io_sem.at[i])
        for i, (a, b) in enumerate(
            (
                (R.dout_hbm, R.dout), (R.hid_hbm, R.hid), (R.w_out_hbm, R.w_out), (R.f_out_hbm, R.f_out), (R.f_in_hbm, R.f_in),
                (R.k.at[:, lanes(src)], R.kh.at[rows(src, 128)]), (R.v.at[:, lanes(src)], R.vh.at[rows(src, 128)]),
                (R.q.at[:, lanes(src)], R.qh.at[src]),
            )
        )
    ]
    for copy in loads:
        copy.start()
    greet(src, tok)

    def by_src(*way):
        return Swap("src", src, *way)

    def by_tok(*way):
        return Swap("tok", tok, *way)

    def first(ref, size=1):
        return lambda n: ref.at[pl.ds(0, n * size)]

    def at(ref):
        return lambda i: ref.at[i]

    def at_rows(ref, size):
        return lambda i: ref.at[rows(i, size)]

    k_swap = by_src(R.k_sem, lambda p: R.k.at[:, lanes(p)], at_rows(R.kh, 128), first(R.kh, 128))
    v_swap = by_src(R.v_sem, lambda p: R.v.at[:, lanes(p)], at_rows(R.vh, 128), first(R.vh, 128))
    q_way = lambda p: R.q.at[:, lanes(p)], at(R.qh), first(R.qh)
    q_near, q_far = by_src(R.qn_sem, *q_way, 1, 4, near_step), by_src(R.qf_sem, *q_way, 4, 8, far_step)
    a_swap = by_src(R.a_sem, at(R.att_send), at(R.att_in), first(R.att_in))
    x_swap = by_tok(R.x_sem, at_rows(R.xs, 16), at_rows(R.xr, 16), first(R.xr, 16))
    g_swap = by_tok(R.g_sem, at_rows(R.gs, 16), at_rows(R.gr, 16), first(R.gr, 16))
    m_swap = by_tok(R.m_sem, at_rows(R.ms, 8), at_rows(R.mr, 8), first(R.mr, 8))
    def xa_half(sem, half):
        return by_src(
            sem, lambda p: R.xall.at[half, rows(src, 32)], lambda i: R.xall.at[half, rows(i, 32)],
            lambda n: R.xall.at[half, pl.ds(0, n * 32)],
        )

    def p_half(sem, half):
        return by_src(
            sem, lambda p: R.part.at[half, rows(p, 32)], lambda i: R.pr.at[i, pl.ds(half * 32, 32)],
            lambda n: R.pr.at[pl.ds(0, n), pl.ds(half * 32, 32)],
        )

    xa_swaps = xa_half(R.xan_sem, 0), xa_half(R.xaf_sem, 1)
    p_swaps = p_half(R.p_sem, 0), p_half(R.p2_sem, 1)
    ga_swap = by_src(
        R.ga_sem, lambda p: R.gall.at[:, rows(src, 32)], lambda i: R.gall.at[:, rows(i, 32)],
        lambda n: R.gall.at[:, pl.ds(0, n * 32)],
    )
    ma_swap = by_src(R.ma_sem, lambda p: R.mall.at[src], at(R.mall), first(R.mall))
    gp_swap = by_src(R.gp_sem, lambda p: R.gps.at[p // 4], at(R.gpr), first(R.gpr))
    b_swap = by_tok(R.b_sem, at_rows(R.ps, 16), at_rows(R.br, 16), first(R.br, 16))
    gb_swap = by_tok(R.gb_sem, lambda p: R.gsum.at[p // 8], at_rows(R.gb, 8), first(R.gb, 8))
    og_way = at(R.og), at(R.ogr), first(R.ogr)
    og_near, og_far = by_src(R.ogn_sem, *og_way, 1, 4, near_step), by_src(R.ogf_sem, *og_way, 4, 8, far_step)
    dq_swap = by_src(R.dq_sem, at(R.dqs), at(R.dqr), first(R.dqr))
    dk_swap = by_src(R.dk_sem, at_rows(R.dks, 128), at(R.dkr), first(R.dkr))
    dv_swap = by_src(R.dv_sem, at_rows(R.dvs, 128), at(R.dvr), first(R.dvr))
    sa_swap = by_src(R.sa_sem, at(R.sa), at(R.sar), first(R.sar))
    sb_swap = by_src(R.sb_sem, at(R.sb), at(R.sbr), first(R.sbr))
    r1_swap = by_tok(R.r1_sem, at(R.r1), at(R.r1r), first(R.r1r))
    r2_swap = by_src(R.r2_sem, lambda p: R.r2.at[src], at(R.r2), first(R.r2))
    r3_swap = by_tok(R.r3_sem, lambda p: R.r3.at[tok], at(R.r3), first(R.r3))
    g1_swap = by_src(R.g1_sem, lambda p: R.g1.at[src], at(R.g1), first(R.g1))
    g2_swap = by_tok(R.g2_sem, lambda p: R.g2.at[tok], at(R.g2), first(R.g2))

    def y_go(sem, source, target, held):
        def send(k):
            to = tok_step(tok, 4 * k)
            remote(source(to // 4), target(y_me), sem.at[0], sem.at[1], "tok", to).start()

        each(4, send)

    def y_arrive(sem, source, target, held):
        bulk_wait(held, sem.at[1])

    def y_sent(sem, source, target, held):
        bulk_wait(held, sem.at[0])

    ya_way = (R.ya_sem, lambda y: R.ya.at[pl.ds(y * 2, 2)], at(R.yar), R.yar.at[pl.ds(0, 3)])
    yb_way = (R.yb_sem, at(R.yb), at(R.ybr), R.ybr.at[pl.ds(0, 3)])

    k_swap.send_all()
    v_swap.send_all()

    def aim_of(id_of, slot_of):
        return jnp.where((id_of < N_TOK) & (slot_of >= 0), id_of * CAP + slot_of, -1)

    j = iota((ROWS, ROWS), 0)
    key = (j // 16) * CAP + j % CAP
    aim_rows = aim_of(R.ids[...], R.slots[...])
    hitT = jnp.where((aim_rows[0:1, :] == key) | (aim_rows[1:2, :] == key), 1.0, 0.0)
    R.hitT[...] = hitT.astype(BF)
    row_blk = (j // CAP) % 4
    zero = jnp.zeros((ROWS, ROWS), BF)

    def to_experts(ref, out):
        acc = None
        for b in range(4):
            term = nn(jnp.where(row_blk == b, R.hitT[...], zero), ref[:, b * 256 : (b + 1) * 256])
            acc = term if acc is None else acc + term
        out[...] = acc.astype(BF)

    loads[0].wait()
    to_experts(R.dout, R.gs)
    g_swap.send_all()
    k_swap.sent_all()
    v_swap.sent_all()
    q_near.send_all()
    q_near.sent_all()
    q_far.send_all()
    R.gr[rows(tok, 16), :] = R.gs[rows(tok, 16), :]
    for copy in loads[5:]:
        copy.wait()
    k_swap.arrive_all()
    v_swap.arrive_all()
    length = R.length[tok]
    seen = iota((SRC_ALL, HEAD), 0) < length
    seen_row = iota((HEAD, SRC_ALL), 1) < length
    k_wide = R.kh[...].astype(F32)
    R.kh[...] = jnp.where(seen, k_wide, k_wide[0:1, :]).astype(BF)
    R.vT[:HEAD, :] = jnp.where(seen_row, R.vh[...].astype(F32).T, 0.0).astype(BF)
    R.vT[HEAD:, :] = jnp.where(seen_row[:16], 1.0, 0.0).astype(BF)

    def forward_block(b):
        q = R.qh[b]
        top = jnp.full((8, ROWS), -3e38, F32)
        for c in range(0, SRC_ALL, 128):
            s = nt(R.kh[c : c + 128, :], q)
            R.sbuf[c : c + 128, :] = s
            top = jnp.maximum(top, fold8(s, jnp.max))
        top = jnp.max(top, axis=0, keepdims=True)
        for c in range(0, SRC_ALL, 128):
            p = jnp.exp2((R.sbuf[c : c + 128, :] - top) * EXP2_SCALE)
            R.pall[b, c : c + 128, :] = p.astype(BF)
        summed = nn(R.vT[...], R.pall[b])
        inv = 1.0 / summed[HEAD : HEAD + 1, :]
        oT = summed[:HEAD, :] * inv
        R.oT[b] = oT.astype(BF)
        R.stat[b] = jnp.broadcast_to(inv, (8, ROWS))
        R.att_send[b] = oT.T.astype(BF)

    i64, j256 = iota((64, ROWS), 0), iota((64, ROWS), 1)
    take = [jnp.where(j256 == (i64 // CAP) * 16 + b * CAP + i64 % CAP, 1.0, 0.0).astype(BF) for b in range(4)]

    def unpack(got, out):
        for b in range(4):
            block = nn(take[b], got[...]).astype(BF)
            out[0, rows(src, 32), b * 256 : (b + 1) * 256] = block[:32]
            out[1, rows(src, 32), b * 256 : (b + 1) * 256] = block[32:]

    def g_on():
        g_swap.arrive_all()
        unpack(R.gr, R.gall)
        ga_swap.send_all()

    forward_block(src)
    R.att_in[src] = R.att_send[src]

    def forward_turn(k):
        forward_block(src_step(src, k, True))
        a_swap.send(src_step(0, k, True))

    q_near.arrive_all()
    each(4, lambda i: forward_turn(near_step(i)))
    q_far.arrive_all()
    each(8, lambda i: forward_turn(far_step(i)), 4)

    id_cols = jnp.concatenate([R.ids[...], R.slots[...], R.ids[...], R.slots[...]], axis=0).astype(F32).T
    id_cols = id_cols.astype(jnp.int32)
    id1, id2, slot1, slot2 = (id_cols[:, i : i + 1] for i in range(4))
    lane = iota((ROWS, HEAD), 1)
    pick1 = jnp.where(id1 == lane, 1.0, 0.0)
    pick2 = jnp.where(id2 == lane, 1.0, 0.0)
    live1, live2 = slot1 >= 0, slot2 >= 0
    base = (src % 4) * 32 + (tok % 8) * CAP
    own1 = jnp.where(live1 & (id1 < N_TOK) & (id1 == lane // 8), 1.0, 0.0)
    own2 = jnp.where(live2 & (id2 < N_TOK) & (id2 == lane // 8), 1.0, 0.0)
    at1 = jnp.where(live1 & (lane == base + slot1), 1.0, 0.0)
    at2 = jnp.where(live2 & (lane == base + slot2), 1.0, 0.0)
    for copy in loads[1:5]:
        copy.wait()
    a_swap.arrive_all()
    for h in range(N_SRC):
        R.att[:, h * HEAD : (h + 1) * HEAD] = R.att_in[h]

    R.mixed[...] = R.hid[...].astype(F32) + nn(R.att[...], R.w_out[...])
    inv_parts = []
    for r in range(0, ROWS, 64):
        m = R.mixed[r : r + 64, :]
        centred = m - jnp.mean(m, axis=1, keepdims=True)
        inv = lax.rsqrt(jnp.mean(centred * centred, axis=1, keepdims=True) + NORM_EPS)
        inv_parts.append(inv)
        normed = centred * inv
        R.mixed[r : r + 64, :] = normed
        R.xin[r : r + 64, :] = (normed * R.gain[...]).astype(BF)
    inv_std = jnp.concatenate(inv_parts, axis=0)
    to_experts(R.xin, R.xs)
    x_swap.send_all()
    g_on()
    R.xr[rows(tok, 16), :] = R.xs[rows(tok, 16), :]
    logits = nn(R.xin[...], R.router[...])
    gap = jnp.sum(logits * (pick1 - pick2), axis=1, keepdims=True)
    gate1 = 1.0 / (1.0 + jnp.exp(-gap))
    gate2 = 1.0 / (1.0 + jnp.exp(gap))
    low1 = gate1.astype(BF).astype(F32)
    low2 = gate2.astype(BF).astype(F32)
    R.ms[...] = nn((own1 * low1).T.astype(BF), at1.astype(BF)) + nn((own2 * low2).T.astype(BF), at2.astype(BF))
    m_swap.send_all()
    R.mr[rows(tok, 8), :] = R.ms[rows(tok, 8), :]
    for swap in (q_far, a_swap, g_swap):
        swap.sent_all()

    x_swap.arrive_all()
    unpack(R.xr, R.xall)
    xa_swaps[0].send_all()
    m_swap.arrive_all()
    R.mall[src] = jnp.concatenate([fold8(R.mr[:64, :], jnp.sum), fold8(R.mr[64:, :], jnp.sum)], axis=0)
    ma_swap.send_all()
    ga_swap.arrive_all()
    for c in range(0, 512, 128):
        R.backT[c : c + 128, :] = nt(R.f_out[c : c + 128, :], R.gall[...].reshape(512, WIDTH))
    R.kT[...] = jnp.where(seen_row, R.kh[...].astype(F32).T, 0.0).astype(BF)
    xa_swaps[0].sent_all()
    xa_swaps[1].send_all()
    for swap in (x_swap, m_swap, ga_swap):
        swap.sent_all()
    ma_swap.arrive_all()

    for half in range(2):
        xa_swaps[half].arrive_all()
        here = slice(half * 256, (half + 1) * 256)
        x_half = R.xall[half]
        gates = jnp.sum(R.mall[:, half * 8 : half * 8 + 8, :].reshape(2, 4, 8, HEAD), axis=1)
        gate_row = jnp.concatenate([gates[0, 0:1, :], gates[1, 0:1, :]], axis=1)
        gate_acc = jnp.zeros((8, 256), F32)
        for c in range(0, 512, 128):
            value, slope = gelu_pair(nt(R.f_in[c : c + 128, :], x_half))
            act = value.astype(BF).astype(F32)
            back = R.backT[c : c + 128, here]
            gate_acc = gate_acc + fold8(back * act, jnp.sum)
            R.actg[c : c + 128, here] = (act * gate_row).astype(BF)
            dp = gate_row * back * slope
            R.dpT[c : c + 128, here] = dp.astype(BF)
            R.dpr[here, c : c + 128] = dp.T.astype(BF)
        gate_tot = jnp.sum(gate_acc, axis=0, keepdims=True)
        R.gps[0, half] = jnp.broadcast_to(gate_tot[:, :HEAD], (8, HEAD))
        R.gps[1, half] = jnp.broadcast_to(gate_tot[:, HEAD:], (8, HEAD))
        R.part[half] = nn(R.dpr[here, :], R.f_in[...]).astype(BF)
        p_swaps[half].send_all()
        R.pr[src, half * 32 : half * 32 + 32, :] = R.part[half, rows(src, 32), :]
    gp_swap.send_all()
    R.gpr[src] = R.gps[src // 4]
    stores = [
        pltpu.make_async_copy(a, b, R.io_sem.at[8 + i])
        for i, (a, b) in enumerate(
            (
                (R.d_fin, R.d_fin_hbm), (R.d_fout, R.d_fout_hbm), (R.dhid, R.dhid_hbm),
                (R.dw, R.dw_hbm), (R.d_router, R.d_router_hbm), (R.d_gain, R.d_gain_hbm),
            )
        )
    ]
    for c in range(0, 512, 128):
        R.d_fin[c : c + 128, :] = nn(R.dpT[c : c + 128, :], R.xall[...].reshape(512, WIDTH)).astype(BF)
        R.d_fout[c : c + 128, :] = nn(R.actg[c : c + 128, :], R.gall[...].reshape(512, WIDTH)).astype(BF)
    stores[0].start()
    stores[1].start()
    for swap in (xa_swaps[1], ma_swap):
        swap.sent_all()
    gp_swap.arrive_all()
    R.gsum[...] = jnp.sum(R.gpr[...], axis=0)
    gb_swap.send_all()
    R.gb[rows(tok, 8), :] = R.gsum[tok // 8]
    p_swaps[0].arrive_all()
    p_swaps[1].arrive_all()
    acc = None
    for b in range(4):
        blk = jnp.sum(R.pr[:, :, b * 256 : (b + 1) * 256].astype(F32), axis=0).astype(BF)
        term = nn(take[b].astype(F32).T.astype(BF), blk)
        acc = term if acc is None else acc + term
    R.ps[...] = acc.astype(BF)
    b_swap.send_all()
    R.br[rows(tok, 16), :] = R.ps[rows(tok, 16), :]

    gb_swap.arrive_all()
    first = jnp.where(lane % 8 == 0, 1.0, 0.0)
    got1 = nn(own1 * first, R.gb[...], precision=lax.Precision.HIGHEST)
    got2 = nn(own2 * first, R.gb[...], precision=lax.Precision.HIGHEST)
    grad1 = jnp.sum(got1 * at1, axis=1, keepdims=True)
    grad2 = jnp.sum(got2 * at2, axis=1, keepdims=True)
    logit_grad = gate1 * gate2 * (grad1 - grad2)
    column = (pick1 - pick2) * logit_grad
    col_hi = column.astype(BF)
    col_lo = (column - col_hi.astype(F32)).astype(BF)
    colT = column.T
    colT_hi = colT.astype(BF)
    colT_lo = (colT - colT_hi.astype(F32)).astype(BF)
    router_part = (nn(colT_hi, R.xin[...]) + nn(colT_lo, R.xin[...])).T.astype(BF)
    for t in range(N_TOK):
        R.r1[t] = router_part[t * 64 : (t + 1) * 64, :]
    r1_swap.send_all()
    R.r1r[tok] = R.r1[tok]
    for swap in (*p_swaps, gp_swap, gb_swap):
        swap.sent_all()
    b_swap.arrive_all()

    scaled_sum = jnp.zeros((ROWS, 1), F32)
    cross_sum = jnp.zeros((ROWS, 1), F32)
    scaled_all = []
    gain_rows = []
    for b in range(4):
        cut = slice(b * 256, (b + 1) * 256)
        mine = jnp.where(row_blk == b, R.hitT[...], zero)
        total = lax.dot_general(mine, R.br[...], (((0,), (0,)), ((), ())), preferred_element_type=F32)
        total = total + nt(col_hi, R.router[cut, :]) + nt(col_lo, R.router[cut, :])
        normed = R.mixed[:, cut]
        row = jnp.sum(total * normed, axis=0, keepdims=True)
        gain_rows += [row[:, :HEAD], row[:, HEAD:]]
        scaled = total * R.gain[:, cut]
        scaled_all.append(scaled)
        scaled_sum = scaled_sum + jnp.sum(scaled, axis=1, keepdims=True)
        cross_sum = cross_sum + jnp.sum(scaled * normed, axis=1, keepdims=True)
    mean1 = scaled_sum * (1.0 / WIDTH)
    mean2 = cross_sum * (1.0 / WIDTH)
    for b in range(4):
        cut = slice(b * 256, (b + 1) * 256)
        R.dhid[:, cut] = (
            R.dout[:, cut].astype(F32) + inv_std * (scaled_all[b] - mean1 - R.mixed[:, cut] * mean2)
        ).astype(BF)
    for h in range(N_SRC):
        R.og[h] = nt(R.dhid[...], R.w_out[h * HEAD : (h + 1) * HEAD, :]).astype(BF)
    og_near.send_all()
    R.g1[src] = jnp.concatenate(gain_rows, axis=0)
    g1_swap.send_all()
    stores[2].start()
    R.ogr[src] = R.og[src]

    for i in range(8):
        cut = slice(i * HEAD, (i + 1) * HEAD)
        w = nn(R.att[:, cut].astype(F32).T.astype(BF), R.dhid[...]).astype(BF)
        R.w1[i, 0] = w[:64]
        R.w1[i, 1] = w[64:]
    core_copy = remote(R.w1.at[:, 1 - c_me], R.c1, R.c_sem.at[0], R.c_sem.at[1], "tok", tok_step(tok, 1))
    core_copy.start()
    og_near.sent_all()
    og_far.send_all()
    R.dka[...] = jnp.zeros_like(R.dka)
    R.dva[...] = jnp.zeros_like(R.dva)

    def backward_block(b):
        q, d_o = R.qh[b], R.ogr[b]
        d_wide = d_o.astype(F32)
        row_term = jnp.sum(d_wide.T * R.oT[b].astype(F32), axis=0, keepdims=True)
        factor = R.stat[b][0:1, :] * FACTOR
        scaled_d = (d_wide * R.stat[b].T[:, 0:1]).astype(BF)
        for c in range(0, SRC_ALL, 128):
            p = R.pall[b, c : c + 128, :].astype(F32)
            dp = nt(R.vh[c : c + 128, :], d_o)
            R.dsbuf[c : c + 128, :] = (p * ((dp - row_term) * factor)).astype(BF)
        R.dqs[b] = nn(R.kT[...], R.dsbuf[...]).T.astype(BF)
        R.dka[...] += nn(R.dsbuf[...], q)
        R.dva[...] += nn(R.pall[b], scaled_d)

    def backward_turn(k):
        backward_block(src_step(src, k, True))
        dq_swap.send(src_step(0, k, True))

    def turns(low, high):
        pick = near_step if high <= 4 else far_step
        each(high, lambda i: backward_turn(pick(i)), low)

    backward_block(src)
    R.dqr[src] = R.dqs[src]
    core_copy.wait_recv()
    for i in range(8):
        piece = R.w1[i, c_me].astype(F32) + R.c1[i].astype(F32)
        R.ya[i] = piece[:, :512].astype(BF)
        R.wtmp[i] = piece[:, 512:]
    y_go(*ya_way)
    for s in range(N_SRC):
        R.sb[s] = jnp.concatenate([R.wtmp[i, s * 8 : (s + 1) * 8, :] for i in range(8)], axis=0).astype(BF)
    sb_swap.send_all()
    R.yar[y_me] = R.ya[pl.ds(y_me * 2, 2)]
    R.sbr[src] = R.sb[src]
    r1_swap.arrive_all()
    R.r2[src] = jnp.sum(R.r1r[...].astype(F32), axis=0).astype(BF)
    r2_swap.send_all()
    og_near.arrive_all()
    turns(1, 4)
    g1_swap.arrive_all()
    R.g2[tok] = jnp.sum(R.g1[...], axis=0)
    g2_swap.send_all()
    r2_swap.arrive_all()
    R.r3[tok] = jnp.sum(R.r2[...].astype(F32), axis=0).astype(BF)
    r3_swap.send_all()
    og_far.arrive_all()
    turns(4, 6)
    y_arrive(*ya_way)
    a0 = jnp.sum(R.yar[:, 0].astype(F32), axis=0)
    a1 = jnp.sum(R.yar[:, 1].astype(F32), axis=0)
    for s in range(N_SRC):
        R.sa[s] = jnp.concatenate([a0[s * 8 : (s + 1) * 8, :], a1[s * 8 : (s + 1) * 8, :]], axis=0).astype(BF)
    sa_swap.send_all()
    R.sar[src] = R.sa[src]
    sb_swap.arrive_all()
    sums = jnp.sum(R.sbr[...].astype(F32), axis=0)
    for y in range(4):
        R.yb[y] = sums[y * 16 : (y + 1) * 16, :].astype(BF)
    y_go(*yb_way)
    R.ybr[y_me] = R.yb[y_me]
    turns(6, 8)
    R.dks[...] = jnp.where(seen, R.dka[...], 0.0).astype(BF)
    dk_swap.send_all()
    R.dvs[...] = jnp.where(seen, R.dva[...], 0.0).astype(BF)
    dv_swap.send_all()
    R.dkr[src] = R.dks[rows(src, 128), :]
    R.dvr[src] = R.dvs[rows(src, 128), :]
    sa_swap.arrive_all()
    y_arrive(*yb_way)
    sums_a = jnp.sum(R.sar[...].astype(F32), axis=0)
    sums_b = jnp.sum(R.ybr[...].astype(F32), axis=0)
    for x in range(2):
        R.x5[x, :, :512] = sums_a[x * 8 : (x + 1) * 8, :]
        R.x5[x, :, 512:] = sums_b[x * 8 : (x + 1) * 8, :]
    x_copy = remote(R.x5.at[1 - x_me], R.x5.at[2], R.xh_sem.at[0], R.xh_sem.at[1], "tok", tok_step(tok, 2))
    x_copy.start()
    for swap in (b_swap, r1_swap, og_far, r2_swap, g1_swap, sb_swap, sa_swap):
        swap.sent_all()
    core_copy.wait_send()
    y_sent(*ya_way)
    y_sent(*yb_way)

    def keep(swap, held, out, sem):
        swap.arrive_all()
        for h in range(N_SRC):
            pltpu.make_async_copy(held.at[h], out.at[:, pl.ds(h * HEAD, HEAD)], sem).start()

    keep(dq_swap, R.dqr, R.dq_hbm, R.io_sem.at[14])
    g2_swap.arrive_all()
    R.d_gain[...] = jnp.sum(R.g2[...], axis=0)
    r3_swap.arrive_all()
    for t in range(N_TOK):
        R.d_router[t * 64 : (t + 1) * 64, :] = R.r3[t].astype(F32)
    stores[4].start()
    stores[5].start()
    x_copy.wait_recv()
    R.dw[...] = R.x5[x_me] + R.x5[2]
    stores[3].start()
    keep(dk_swap, R.dkr, R.dk_hbm, R.io_sem.at[15])
    keep(dv_swap, R.dvr, R.dv_hbm, R.io_sem.at[16])
    for swap in (r3_swap, g2_swap, dq_swap, dk_swap, dv_swap):
        swap.sent_all()
    x_copy.wait_send()
    bulk_wait(R.dqr, R.io_sem.at[14])
    bulk_wait(R.dkr, R.io_sem.at[15])
    bulk_wait(R.dvr, R.io_sem.at[16])
    for copy in stores:
        copy.wait()


def hand_over_kernel(*refs):
    count = (len(refs) - 1) // 3
    given, out, held, sem = refs[:count], refs[count : 2 * count], refs[2 * count : 3 * count], refs[-1]
    order = sorted(range(count), key=lambda i: -given[i].size)
    loads = [pltpu.make_async_copy(given[i], held[i], sem.at[0, i]) for i in order]
    stores = [pltpu.make_async_copy(held[i], out[i], sem.at[1, i]) for i in order]
    for copy in loads:
        copy.start()
    for load, store in zip(loads, stores):
        load.wait()
        store.start()
    for copy in stores:
        copy.wait()


VMEM = pl.BlockSpec(memory_space=pltpu.VMEM)
SMEM = pl.BlockSpec(memory_space=pltpu.SMEM)
HBM = pl.BlockSpec(memory_space=pl.ANY)


def on_device(
    hidden_in, d_out, queries, keys, values, source_len, out_weight, norm_gain, router,
    expert_ids, expert_slots, fc_in, fc_out,
):
    shapes = tuple(
        jax.ShapeDtypeStruct(s, d)
        for s, d in (
            ((ROWS, WIDTH), BF), ((ROWS, WIDTH), BF), ((HEAD, WIDTH), BF), ((HEAD, WIDTH), BF), ((8, WIDTH), F32),
            ((WIDTH, HEAD), F32), ((8, HEAD), F32), ((512, WIDTH), BF), ((512, WIDTH), BF),
        )
    )
    outs = pl.pallas_call(
        block_kernel,
        out_shape=shapes,
        in_specs=[SMEM] + [VMEM] * 4 + [HBM] * 8,
        out_specs=(HBM,) * 9,
        scratch_shapes=list(SCRATCH.values()),
        compiler_params=pltpu.CompilerParams(
            collective_id=1, has_side_effects=True, vmem_limit_bytes=58 * 1024 * 1024
        ),
    )(
        source_len, norm_gain[None], router, expert_ids.T, expert_slots.T, queries, keys[0], values[0], d_out,
        hidden_in, out_weight, fc_in[0], fc_out[0],
    )
    dhid, dq, dk, dv, dw, d_router, d_gain, d_fin, d_fout = pl.pallas_call(
        hand_over_kernel,
        out_shape=shapes,
        in_specs=[HBM] * 9,
        out_specs=(HBM,) * 9,
        scratch_shapes=[pltpu.VMEM(s.shape, s.dtype) for s in shapes] + [sems(2, 9)],
        compiler_params=pltpu.CompilerParams(vmem_limit_bytes=58 * 1024 * 1024),
    )(*outs)
    return dhid, dq, dk[None], dv[None], dw, d_router, d_gain.reshape(-1), d_fin[None], d_fout[None]


def solution(mesh):
    return jax.shard_map(
        on_device,
        mesh=mesh,
        in_specs=(
            P(("tok", "src"), None), P(("tok", "src"), None), P(("tok", "src"), None),
            P("tok", "src", None), P("tok", "src", None), P(), P(), P(), P(),
            P(("tok", "src"), None), P(("tok", "src"), None), P("tok", "src", None), P("tok", "src", None),
        ),
        out_specs=(
            P(("tok", "src"), None), P(("tok", "src"), None), P("tok", "src", None), P("tok", "src", None),
            P(("tok", "src"), None), P(), P(), P("tok", "src", None), P("tok", "src", None),
        ),
        check_vma=False,
    )
```
